32 devices in a mesh: dp: 4 (over y, x), expert: 8 (over z, core).
Axes of the slice: x: 2, y: 2, z: 4, core: 2. Of those that a mesh axis runs over, the one named last changes fastest.
Arguments:
- unit_codes: bfloat16 [16, 256, 1536], P('expert', 'dp'), may hold values from -4 to 4
- block_scales: float32 [16, 12, 256], P('expert', None, 'dp'), may hold values from 0.05 to 2
- pair_list: int32 [32, 2], replicated, may hold values from 0 to 15, as said below
Outputs:
- left_best: float32 [8, 4, 1536], P('expert', None, 'dp')
- right_best: float32 [8, 4, 1536], P('expert', None, 'dp')
The draws below stay inside these ranges and needn't reach their ends.
Inputs may be any that keep to these rules, and one draw needn't show every extreme that they name: `pair_list`: row 4 * e + s names as its first expert one of 2 * e to 2 * e + 1, and as its second one of the 2 experts starting at 2 * ((e + o_s) mod n), with n = 8; the offsets o_s are nonzero, distinct over s, include 1, n / 2 and n - 1, and are the same for every e.
All inputs are finite; a program needn't handle non-finite values.
Results may differ from the reference program's by a relative error of at most 0.0017.
Values may be sent and summed in bfloat16 or wider, within the bound.
A program may use at most 128 MiB of HBM per device.

```python
import math
import jax
import jax.numpy as jnp
from jax import lax

FF = 1536
EXP_DEV = 2
SCALE_BLOCK = 128
EXPERTS = 16
CAL_ROWS = 256
PAIR_DEV = 4
PAIRS = 32
N_EXPERT = 8


def draw_pair_list(key, part):
    num_devices = EXPERTS // EXP_DEV
    key_offsets = jax.random.fold_in(key, 11)
    key_left = jax.random.fold_in(key, 12)
    key_right = jax.random.fold_in(key, 13)
    key_order = jax.random.fold_in(key, 14)
    values = jnp.arange(1, num_devices, dtype=jnp.int32)
    ranks = jax.random.permutation(key_offsets, num_devices - 1).astype(jnp.int32)
    ranks = jnp.where(values == 1, -3, ranks)
    ranks = jnp.where(values == num_devices // 2, -2, ranks)
    ranks = jnp.where(values == num_devices - 1, -1, ranks)
    order = jnp.argsort(ranks, stable=True)
    picked = jnp.take(values, order[:PAIR_DEV])
    offsets = jax.random.permutation(key_order, picked)
    device_ids = jnp.arange(num_devices, dtype=jnp.int32)[:, None]
    left_pick = jax.random.randint(key_left, (num_devices, PAIR_DEV), 0, EXP_DEV)
    left_pick = left_pick.at[:, 0].set(0).at[:, 1].set(EXP_DEV - 1)
    right_pick = jax.random.randint(key_right, (num_devices, PAIR_DEV), 0, EXP_DEV)
    first_expert = device_ids * EXP_DEV + left_pick
    second_expert = (device_ids + offsets[None, :]) % num_devices * EXP_DEV + right_pick
    stacked = jnp.stack([first_expert, second_expert], axis=-1)
    return stacked.reshape(PAIRS, 2).astype(jnp.int32)


def block_scale(own_key, extent, pieces, low, top_value):
    level = 1.0
    for axis_at, blocks in pieces:
        draws = jax.random.uniform(jax.random.fold_in(jax.random.fold_in(own_key, 6), axis_at), (blocks,), jnp.float32, low / len(pieces), top_value / len(pieces))
        level = level * jnp.repeat(jnp.exp(draws), extent[axis_at] // blocks).reshape((-1,) + (1,) * (len(extent) - 1 - axis_at))
    return level


def scatter_about(rng, shape, deviation, limit, cuts=(), held_as=jnp.bfloat16):
    entries = deviation * jax.random.normal(rng, shape, jnp.float32)
    if cuts:
        entries = entries * block_scale(rng, shape, cuts, -0.22, 0.18)
    return jnp.clip(entries, -limit, limit).astype(held_as)


def setup_inputs(seed: int = 0) -> dict:
    key_list = jax.random.split(jax.random.key(seed), 4)
    return {
        "unit_codes": scatter_about(key_list[0], (EXPERTS, CAL_ROWS, FF), 1.0, 4.0, ((0, 8), (1, 4))),
        "block_scales": jnp.clip(jnp.exp(math.log(2.0) - 3.6888794 * jax.random.uniform(key_list[1], (EXPERTS, FF // SCALE_BLOCK, CAL_ROWS), jnp.float32) ** block_scale(key_list[1], (EXPERTS, FF // SCALE_BLOCK, CAL_ROWS), ((0, 8), (2, 4)), -0.2, 0.2)), 0.05, 2.0),
        "pair_list": draw_pair_list(jax.random.fold_in(key_list[3], 71), 0),
    }


EPSILON = 1e-06

def reference(unit_codes, block_scales, pair_list):
    expanded = jnp.repeat(jnp.transpose(block_scales, (0, 2, 1)), SCALE_BLOCK, axis=2)
    acts = (unit_codes.astype(jnp.float32) * expanded).astype(jnp.bfloat16)
    acts_wide = acts.astype(jnp.float32)
    mean_square = lax.optimization_barrier(jnp.mean(acts_wide * acts_wide, axis=1))
    inverse = 1.0 / jnp.sqrt(mean_square + EPSILON)

    def single(pair_row):
        first_expert = pair_row[0]
        second_expert = pair_row[1]
        first_rows = jnp.take(acts_wide, first_expert, axis=0)
        second_rows = jnp.take(acts_wide, second_expert, axis=0)
        products = jnp.dot(first_rows.T, second_rows, precision=lax.Precision.HIGHEST, preferred_element_type=jnp.float32)
        correlation = products / CAL_ROWS * jnp.take(inverse, first_expert, axis=0)[:, None] * jnp.take(inverse, second_expert, axis=0)[None, :]
        return (lax.optimization_barrier(jnp.max(correlation, axis=1)), lax.optimization_barrier(jnp.max(correlation, axis=0)))
    left_rows, right_rows = lax.map(single, pair_list)
    left_best = left_rows.reshape(N_EXPERT, PAIR_DEV, FF)
    offsets = pair_list[:PAIR_DEV, 1] // EXP_DEV
    devices = jnp.arange(N_EXPERT, dtype=jnp.int32)[:, None]
    source_dev = (devices - offsets[None, :]) % N_EXPERT
    lookup = (source_dev * PAIR_DEV + jnp.arange(PAIR_DEV, dtype=jnp.int32)[None, :]).astype(jnp.int32)
    right_best = jnp.take(right_rows, lookup.reshape(-1), axis=0).reshape(N_EXPERT, PAIR_DEV, FF)
    return (left_best, right_best)
```

```python
import functools
import itertools
import math

import jax
import jax.numpy as jnp
from jax import lax
from jax.experimental import pallas as pl
from jax.experimental.pallas import tpu as pltpu
from jax.sharding import PartitionSpec as P

EPSILON = 1e-06


def general_body(unit_codes, block_scales, pair_list):
    num_devices = lax.axis_size("expert")
    groups = lax.axis_size("dp")
    my_index = lax.axis_index("expert")
    dp_index = lax.axis_index("dp")
    per_device, row_count, unit_count = unit_codes.shape
    num_blocks = block_scales.shape[1]
    block_len = unit_count // num_blocks
    slice_width = unit_count // groups
    factor = jnp.transpose(block_scales, (0, 2, 1))[:, :, :, None]
    acts = (
        unit_codes.astype(jnp.float32).reshape(per_device, row_count, num_blocks, block_len)
        * factor
    )
    acts = acts.reshape(per_device, row_count, unit_count).astype(jnp.bfloat16)
    slot_count = pair_list.shape[0] // num_devices
    pair_table = pair_list.reshape(num_devices, slot_count, 2)
    my_pairs = lax.dynamic_index_in_dim(pair_table, my_index, 0, keepdims=False)
    left_local = my_pairs[:, 0] % per_device
    right_dev = my_pairs[:, 1] // per_device
    is_asked = pair_table[:, :, 1] // per_device == my_index
    chosen = jnp.sum(jnp.where(is_asked, pair_table[:, :, 1] % per_device, 0), axis=1)
    in_use = jnp.any(is_asked, axis=1)
    chooser = ((chosen[:, None] == jnp.arange(per_device)[None, :]) & in_use[:, None]).astype(
        jnp.bfloat16
    )
    own_full = lax.all_gather(acts, "dp", axis=1, tiled=True)
    flattened = acts.reshape(per_device, -1)
    outbound = jnp.dot(chooser, flattened, preferred_element_type=jnp.float32).astype(jnp.bfloat16)
    received = lax.all_to_all(
        outbound.reshape((num_devices,) + acts.shape[1:]),
        "expert",
        split_axis=0,
        concat_axis=0,
        tiled=True,
    )
    wanted = jnp.take(received, right_dev, axis=0)
    partner = lax.all_to_all(wanted, "dp", split_axis=2, concat_axis=1, tiled=True)
    all_rows = partner.shape[1]
    own_square = (
        jnp.einsum("era,era->ea", own_full, own_full, preferred_element_type=jnp.float32) / all_rows
    )
    inv_own = 1.0 / jnp.sqrt(own_square + EPSILON)
    part_square = (
        jnp.einsum("srb,srb->sb", partner, partner, preferred_element_type=jnp.float32) / all_rows
    )
    inv_part = 1.0 / jnp.sqrt(part_square + EPSILON)

    def single(member):
        expert_pick, partner_block, inv_unit = member
        left_rows = jnp.take(own_full, expert_pick, axis=0)
        gram_block = jnp.einsum(
            "ra,rb->ab", left_rows, partner_block, preferred_element_type=jnp.float32
        )
        correlation = (
            gram_block
            / all_rows
            * jnp.take(inv_own, expert_pick, axis=0)[:, None]
            * inv_unit[None, :]
        )
        return (jnp.max(correlation, axis=1), jnp.max(correlation, axis=0))

    def several(member):
        return jax.vmap(single)(member)

    bundle = math.gcd(slot_count, 4)
    stacked = (
        left_local.reshape(-1, bundle),
        partner.reshape(-1, bundle, all_rows, slice_width),
        inv_part.reshape(-1, bundle, slice_width),
    )
    left_part, right_part = lax.map(several, stacked)
    left_part = left_part.reshape(slot_count, unit_count)
    right_part = right_part.reshape(slot_count, slice_width)
    left_all = lax.pmax(left_part, "dp")
    left_out = lax.dynamic_slice_in_dim(left_all, dp_index * slice_width, slice_width, 1)
    target = (right_dev[:, None] == jnp.arange(num_devices)[None, :]).astype(jnp.float32)
    outgoing = jnp.dot(
        target.T, right_part, precision=lax.Precision.HIGHEST, preferred_element_type=jnp.float32
    )
    returned = lax.all_to_all(outgoing, "expert", split_axis=0, concat_axis=0, tiled=True)
    offsets = pair_table[0, :, 1] // per_device
    source_dev = (my_index - offsets) % num_devices
    right_out = jnp.take(returned, source_dev, axis=0)
    return (left_out[None], right_out[None])


MESH = pl.DeviceIdType.MESH
CHUNK = 256
MAX_BRANCHES = 8
TURNS = {
    (1, 2, 4, 7): ((1, 7, 4, 2), (1, 1, 2, 2, 0, 3, 1, 0)),
    (1, 3, 4, 7): ((1, 4, 7, 3), (0, 1, 3, 0, 3, 1, 2, 0)),
    (1, 4, 5, 7): ((1, 4, 7, 5), (0, 0, 1, 3, 3, 2, 1, 2)),
    (1, 4, 6, 7): ((1, 7, 6, 4), (0, 2, 1, 3, 2, 3, 3, 0)),
}


def pick(index, table):
    total = 0
    size = len(table)
    for at, value in enumerate(table):
        if value:
            apart = (index - at) * (index - at)
            total = total + value * (1 - (apart + size * size - 1) // (size * size))
    return total


def pair_kernel(
    order, turns, n, groups,
    codes_ref, scales_ref, pairs_ref, left_out, right_out,
    acts, send_left, send_right, left_rows, right_rows, turned, inv_left, best, right_row,
    left_stage, right_stage, left_got, right_got,
    left_send_sem, left_sem, right_send_sem, right_sem, out_send_sem, left_got_sem, right_got_sem,
):
    me = lax.axis_index("expert")
    dp = lax.axis_index("dp")
    per_device, rows, units = codes_ref.shape
    blocks = scales_ref.shape[1]
    width = units // blocks
    chunks = units // CHUNK
    part = units // groups
    all_rows = groups * rows

    def share_of(member, column):
        return (member - pick(column, turns) + groups) % groups

    def member_of(share, column):
        return (share + pick(column, turns)) % groups

    mine = share_of(dp, me)
    my_offset = pick(mine, order)
    partner = (me + my_offset) % n
    askers = [(me - order[k] + n) % n for k in range(groups)]
    ask_member = [member_of(k, askers[k]) for k in range(groups)]
    others = [(dp + r) % groups for r in range(1, groups)]

    barrier = pltpu.get_barrier_semaphore()
    greeted = [(other, me) for other in others]
    greeted += [(ask_member[k], askers[k]) for k in range(groups)]
    greeted += [(member, partner) for member in range(groups)]
    for device in greeted:
        pl.semaphore_signal(barrier, inc=1, device_id=device, device_id_type=MESH)

    for expert in range(per_device):
        factor = scales_ref[expert].T
        for block in range(blocks):
            at = slice(block * width, (block + 1) * width)
            acts[expert, :, at] = (
                codes_ref[expert, :, at].astype(jnp.float32) * factor[:, block : block + 1]
            ).astype(jnp.bfloat16)

    def slot_of(offset):
        slot = 0
        for s in range(groups):
            slot = slot + jnp.where(pairs_ref[2 * s + 1] // per_device == offset, s, 0)
        return slot

    def chosen(column, slot, side):
        return lax.rem(pairs_ref[2 * (groups * column + slot) + side], per_device)

    for k in range(groups):
        held = acts[chosen(askers[k], slot_of(order[k]), 1)]
        for c in range(chunks):
            send_right[k, c] = held[:, c * CHUNK : (c + 1) * CHUNK]
    for r, other in enumerate(others):
        offset = pick(share_of(other, me), order)
        send_left[r] = acts[chosen(me, slot_of(offset), 0)]
    my_rows = pl.ds(pl.multiple_of(dp * rows, rows), rows)
    left_rows[my_rows, :] = acts[chosen(me, slot_of(my_offset), 0)]

    def left_copy(r):
        return pltpu.make_async_remote_copy(
            src_ref=send_left.at[r],
            dst_ref=left_rows.at[my_rows, :],
            send_sem=left_send_sem.at[r],
            recv_sem=left_sem.at[dp],
            device_id=(others[r], me),
            device_id_type=MESH,
        )

    def right_copy(k, c):
        return pltpu.make_async_remote_copy(
            src_ref=send_right.at[k, c],
            dst_ref=right_rows.at[c, my_rows, :],
            send_sem=right_send_sem.at[k, c],
            recv_sem=right_sem.at[c, dp],
            device_id=(ask_member[k], askers[k]),
            device_id_type=MESH,
        )

    pl.semaphore_wait(barrier, len(greeted))
    for r in range(groups - 1):
        left_copy(r).start()

    @pl.loop(0, chunks)
    def _(c):
        for k in range(groups):
            right_copy(k, c).start()

    best[...] = jnp.full_like(best, -jnp.inf)
    for other in others:
        theirs = pl.ds(pl.multiple_of(other * rows, rows), rows)
        pltpu.make_async_remote_copy(
            src_ref=send_left.at[0],
            dst_ref=left_rows.at[theirs, :],
            send_sem=left_send_sem.at[0],
            recv_sem=left_sem.at[other],
            device_id=(other, me),
            device_id_type=MESH,
        ).wait_recv()

    for i in range(chunks):
        at = slice(i * CHUNK, (i + 1) * CHUNK)
        block = left_rows[:, at]
        wide = block.astype(jnp.float32)
        square = jnp.sum(wide * wide, axis=0, keepdims=True) / all_rows
        inverse = 1.0 / jnp.sqrt(square + EPSILON)
        inv_left[at, :] = jnp.broadcast_to(inverse, (128, CHUNK)).T
        turned[at, :] = block.T

    @pl.loop(0, chunks)
    def _(c):
        for member in range(groups):
            pltpu.make_async_remote_copy(
                src_ref=send_right.at[0, 0],
                dst_ref=right_rows.at[c, pl.ds(member * rows, rows), :],
                send_sem=right_send_sem.at[0, 0],
                recv_sem=right_sem.at[c, member],
                device_id=(member, partner),
                device_id_type=MESH,
            ).wait_recv()
        block = right_rows[c]
        wide = block.astype(jnp.float32)
        square = jnp.sum(wide * wide, axis=0, keepdims=True) / all_rows
        inverse = 1.0 / jnp.sqrt(square + EPSILON)
        tops = [jnp.full((8, 128), -jnp.inf, jnp.float32) for _ in range(CHUNK // 128)]
        for i in range(chunks):
            at = slice(i * CHUNK, (i + 1) * CHUNK)
            gram = jnp.dot(turned[at, :], block, preferred_element_type=jnp.float32)
            scale = inv_left[at, :]
            running = best[at, :]
            for h in range(CHUNK // 128):
                lanes = slice(h * 128, (h + 1) * 128)
                scaled = gram[:, lanes] * scale
                running = jnp.maximum(running, scaled * inverse[:, lanes])
                gram_top = jnp.max(scaled.reshape(CHUNK // 8, 8, 128), axis=0)
                tops[h] = jnp.maximum(tops[h], gram_top)
            best[at, :] = running
        top = jnp.max(jnp.concatenate(tops, axis=1), axis=0, keepdims=True)
        right_row[c] = top * inverse / all_rows

    right_full = jnp.concatenate([right_row[c] for c in range(chunks)], axis=1)
    left_full = jnp.concatenate(
        [
            jnp.max(best[i * CHUNK : (i + 1) * CHUNK, :].T, axis=0, keepdims=True)
            for i in range(chunks)
        ],
        axis=1,
    ) / all_rows
    for member in range(groups):
        at = slice(member * part, (member + 1) * part)
        right_stage[member] = right_full[:, at]
        left_stage[member] = left_full[:, at]

    def right_result(member):
        return pltpu.make_async_remote_copy(
            src_ref=right_stage.at[member],
            dst_ref=right_got.at[mine],
            send_sem=out_send_sem.at[member],
            recv_sem=right_got_sem.at[mine],
            device_id=(member, partner),
            device_id_type=MESH,
        )

    def left_result(r):
        return pltpu.make_async_remote_copy(
            src_ref=left_stage.at[others[r]],
            dst_ref=left_got.at[mine],
            send_sem=out_send_sem.at[groups + r],
            recv_sem=left_got_sem.at[mine],
            device_id=(others[r], me),
            device_id_type=MESH,
        )

    for member in range(groups):
        right_result(member).start()
    for r in range(groups - 1):
        left_result(r).start()
    left_got[mine] = left_stage[dp]

    for r in range(groups - 1):
        left_copy(r).wait_send()

    @pl.loop(0, chunks)
    def _(c):
        for k in range(groups):
            right_copy(k, c).wait_send()

    for other in others:
        share = share_of(other, me)
        pltpu.make_async_remote_copy(
            src_ref=left_stage.at[0],
            dst_ref=left_got.at[share],
            send_sem=out_send_sem.at[0],
            recv_sem=left_got_sem.at[share],
            device_id=(other, me),
            device_id_type=MESH,
        ).wait_recv()
    for k in range(groups):
        pltpu.make_async_remote_copy(
            src_ref=right_stage.at[0],
            dst_ref=right_got.at[k],
            send_sem=out_send_sem.at[0],
            recv_sem=right_got_sem.at[k],
            device_id=(ask_member[k], askers[k]),
            device_id_type=MESH,
        ).wait_recv()
    for member in range(groups):
        right_result(member).wait_send()
    for r in range(groups - 1):
        left_result(r).wait_send()

    for s in range(groups):
        offset = pairs_ref[2 * s + 1] // per_device
        share = 0
        for k in range(groups):
            share = share + jnp.where(offset == order[k], k, 0)
        left_out[0, s : s + 1, :] = left_got[share]
        right_out[0, s : s + 1, :] = right_got[share]


def pair_call(order, turns, n, groups, collective_id, unit_codes, block_scales, pairs):
    per_device, rows, units = unit_codes.shape
    chunks = units // CHUNK
    part = units // groups
    out = jax.ShapeDtypeStruct((1, groups, part), jnp.float32)
    vmem = pl.BlockSpec(memory_space=pltpu.VMEM)
    dma = pltpu.SemaphoreType.DMA
    return pl.pallas_call(
        functools.partial(pair_kernel, order, turns, n, groups),
        out_shape=(out, out),
        in_specs=[vmem, vmem, pl.BlockSpec(memory_space=pltpu.SMEM)],
        out_specs=(vmem, vmem),
        scratch_shapes=[
            pltpu.VMEM((per_device, rows, units), jnp.bfloat16),
            pltpu.VMEM((groups - 1, rows, units), jnp.bfloat16),
            pltpu.VMEM((groups, chunks, rows, CHUNK), jnp.bfloat16),
            pltpu.VMEM((groups * rows, units), jnp.bfloat16),
            pltpu.VMEM((chunks, groups * rows, CHUNK), jnp.bfloat16),
            pltpu.VMEM((units, groups * rows), jnp.bfloat16),
            pltpu.VMEM((units, 128), jnp.float32),
            pltpu.VMEM((units, 128), jnp.float32),
            pltpu.VMEM((chunks, 1, CHUNK), jnp.float32),
            pltpu.VMEM((groups, 1, part), jnp.float32),
            pltpu.VMEM((groups, 1, part), jnp.float32),
            pltpu.VMEM((groups, 1, part), jnp.float32),
            pltpu.VMEM((groups, 1, part), jnp.float32),
            dma((groups - 1,)),
            dma((groups,)),
            dma((groups, chunks)),
            dma((chunks, groups)),
            dma((2 * groups - 1,)),
            dma((groups,)),
            dma((groups,)),
        ],
        compiler_params=pltpu.CompilerParams(
            collective_id=collective_id, has_side_effects=True, vmem_limit_bytes=24 * 2**20
        ),
        cost_estimate=pl.CostEstimate(
            flops=2 * units * units * groups * rows, bytes_accessed=2 * units * rows * per_device, transcendentals=0
        ),
    )(unit_codes, block_scales, pairs)


def offset_sets(n, slots):
    fixed = sorted({1, n // 2, n - 1})
    rest = [o for o in range(1, n) if o not in fixed]
    free = slots - len(fixed)
    if free < 0 or math.comb(len(rest), free) > MAX_BRANCHES:
        return []
    return [tuple(sorted(fixed + list(more))) for more in itertools.combinations(rest, free)]


def body(unit_codes, block_scales, pair_list):
    n = lax.axis_size("expert")
    groups = lax.axis_size("dp")
    per_device, rows, units = unit_codes.shape
    slots = pair_list.shape[0] // n
    sets = offset_sets(n, slots)
    fits = (
        slots == groups
        and rows % 16 == 0
        and units % CHUNK == 0
        and units % (128 * groups) == 0
        and (groups * rows) % 128 == 0
    )
    if not sets or not fits:
        return general_body(unit_codes, block_scales, pair_list)
    offsets = pair_list[:slots, 1] // per_device
    branch = 0
    for at, members in enumerate(sets):
        same = sum(members) == jnp.sum(offsets)
        if len({sum(m) for m in sets}) < len(sets):
            same = jnp.all(jnp.any(offsets[:, None] == jnp.asarray(members)[None, :], axis=1))
        branch = branch + jnp.where(same, at, 0)
    calls = []
    for at, members in enumerate(sets):
        order, turns = TURNS.get(members, (members, (0,) * n)) if (n, groups) == (8, 4) else (members, (0,) * n)
        calls.append(functools.partial(pair_call, order, turns, n, groups, at))
    return lax.switch(branch, calls, unit_codes, block_scales, pair_list.reshape(-1))


def solution(mesh):
    in_specs = (P("expert", "dp", None), P("expert", None, "dp"), P())
    out_specs = (P("expert", None, "dp"), P("expert", None, "dp"))
    return jax.shard_map(body, mesh=mesh, in_specs=in_specs, out_specs=out_specs, check_vma=False)
```

```python
import functools
import itertools
import math

import jax
import jax.numpy as jnp
from jax import lax
from jax.experimental import pallas as pl
from jax.experimental.pallas import tpu as pltpu
from jax.sharding import PartitionSpec as P

EPSILON = 1e-06


def general_body(unit_codes, block_scales, pair_list):
    num_devices = lax.axis_size("expert")
    groups = lax.axis_size("dp")
    my_index = lax.axis_index("expert")
    dp_index = lax.axis_index("dp")
    per_device, row_count, unit_count = unit_codes.shape
    num_blocks = block_scales.shape[1]
    block_len = unit_count // num_blocks
    slice_width = unit_count // groups
    factor = jnp.transpose(block_scales, (0, 2, 1))[:, :, :, None]
    acts = (
        unit_codes.astype(jnp.float32).reshape(per_device, row_count, num_blocks, block_len)
        * factor
    )
    acts = acts.reshape(per_device, row_count, unit_count).astype(jnp.bfloat16)
    slot_count = pair_list.shape[0] // num_devices
    pair_table = pair_list.reshape(num_devices, slot_count, 2)
    my_pairs = lax.dynamic_index_in_dim(pair_table, my_index, 0, keepdims=False)
    left_local = my_pairs[:, 0] % per_device
    right_dev = my_pairs[:, 1] // per_device
    is_asked = pair_table[:, :, 1] // per_device == my_index
    chosen = jnp.sum(jnp.where(is_asked, pair_table[:, :, 1] % per_device, 0), axis=1)
    in_use = jnp.any(is_asked, axis=1)
    chooser = ((chosen[:, None] == jnp.arange(per_device)[None, :]) & in_use[:, None]).astype(
        jnp.bfloat16
    )
    own_full = lax.all_gather(acts, "dp", axis=1, tiled=True)
    flattened = acts.reshape(per_device, -1)
    outbound = jnp.dot(chooser, flattened, preferred_element_type=jnp.float32).astype(jnp.bfloat16)
    received = lax.all_to_all(
        outbound.reshape((num_devices,) + acts.shape[1:]),
        "expert",
        split_axis=0,
        concat_axis=0,
        tiled=True,
    )
    wanted = jnp.take(received, right_dev, axis=0)
    partner = lax.all_to_all(wanted, "dp", split_axis=2, concat_axis=1, tiled=True)
    all_rows = partner.shape[1]
    own_square = (
        jnp.einsum("era,era->ea", own_full, own_full, preferred_element_type=jnp.float32) / all_rows
    )
    inv_own = 1.0 / jnp.sqrt(own_square + EPSILON)
    part_square = (
        jnp.einsum("srb,srb->sb", partner, partner, preferred_element_type=jnp.float32) / all_rows
    )
    inv_part = 1.0 / jnp.sqrt(part_square + EPSILON)

    def single(member):
        expert_pick, partner_block, inv_unit = member
        left_rows = jnp.take(own_full, expert_pick, axis=0)
        gram_block = jnp.einsum(
            "ra,rb->ab", left_rows, partner_block, preferred_element_type=jnp.float32
        )
        correlation = (
            gram_block
            / all_rows
            * jnp.take(inv_own, expert_pick, axis=0)[:, None]
            * inv_unit[None, :]
        )
        return (jnp.max(correlation, axis=1), jnp.max(correlation, axis=0))

    def several(member):
        return jax.vmap(single)(member)

    bundle = math.gcd(slot_count, 4)
    stacked = (
        left_local.reshape(-1, bundle),
        partner.reshape(-1, bundle, all_rows, slice_width),
        inv_part.reshape(-1, bundle, slice_width),
    )
    left_part, right_part = lax.map(several, stacked)
    left_part = left_part.reshape(slot_count, unit_count)
    right_part = right_part.reshape(slot_count, slice_width)
    left_all = lax.pmax(left_part, "dp")
    left_out = lax.dynamic_slice_in_dim(left_all, dp_index * slice_width, slice_width, 1)
    target = (right_dev[:, None] == jnp.arange(num_devices)[None, :]).astype(jnp.float32)
    outgoing = jnp.dot(
        target.T, right_part, precision=lax.Precision.HIGHEST, preferred_element_type=jnp.float32
    )
    returned = lax.all_to_all(outgoing, "expert", split_axis=0, concat_axis=0, tiled=True)
    offsets = pair_table[0, :, 1] // per_device
    source_dev = (my_index - offsets) % num_devices
    right_out = jnp.take(returned, source_dev, axis=0)
    return (left_out[None], right_out[None])


MESH = pl.DeviceIdType.MESH
CHUNK = 256
MAX_BRANCHES = 8
TURNS = {
    (1, 2, 4, 7): ((1, 7, 4, 2), (1, 1, 2, 2, 0, 3, 1, 0)),
    (1, 3, 4, 7): ((1, 4, 7, 3), (0, 1, 3, 0, 3, 1, 2, 0)),
    (1, 4, 5, 7): ((1, 4, 7, 5), (0, 0, 1, 3, 3, 2, 1, 2)),
    (1, 4, 6, 7): ((1, 7, 6, 4), (0, 2, 1, 3, 2, 3, 3, 0)),
}


def pick(index, table):
    total = 0
    size = len(table)
    for at, value in enumerate(table):
        if value:
            apart = (index - at) * (index - at)
            total = total + value * (1 - (apart + size * size - 1) // (size * size))
    return total


def pair_kernel(
    order, turns, n, groups,
    codes_ref, scales_ref, pairs_ref, left_out, right_out,
    acts, send_left, send_right, left_rows, right_rows, turned, inv_left, best, right_row,
    left_stage, right_stage, left_got, right_got,
    left_send_sem, left_sem, right_send_sem, right_sem, out_send_sem, left_got_sem, right_got_sem,
):
    me = lax.axis_index("expert")
    dp = lax.axis_index("dp")
    per_device, rows, units = codes_ref.shape
    blocks = scales_ref.shape[1]
    width = units // blocks
    chunks = units // CHUNK
    part = units // groups
    all_rows = groups * rows

    def share_of(member, column):
        return (member - pick(column, turns) + groups) % groups

    def member_of(share, column):
        return (share + pick(column, turns)) % groups

    mine = share_of(dp, me)
    my_offset = pick(mine, order)
    partner = (me + my_offset) % n
    askers = [(me - order[k] + n) % n for k in range(groups)]
    ask_member = [member_of(k, askers[k]) for k in range(groups)]
    others = [(dp + r) % groups for r in range(1, groups)]

    barrier = pltpu.get_barrier_semaphore()
    greeted = [(other, me) for other in others]
    greeted += [(ask_member[k], askers[k]) for k in range(groups)]
    greeted += [(member, partner) for member in range(groups)]
    for device in greeted:
        pl.semaphore_signal(barrier, inc=1, device_id=device, device_id_type=MESH)

    for expert in range(per_device):
        factor = scales_ref[expert].T
        for block in range(blocks):
            at = slice(block * width, (block + 1) * width)
            acts[expert, :, at] = (
                codes_ref[expert, :, at].astype(jnp.float32) * factor[:, block : block + 1]
            ).astype(jnp.bfloat16)

    def slot_of(offset):
        slot = 0
        for s in range(groups):
            slot = slot + jnp.where(pairs_ref[1, s] // per_device == offset, s, 0)
        return slot

    def chosen(column, slot, side):
        return lax.rem(pairs_ref[side, groups * column + slot], per_device)

    for k in range(groups):
        held = acts[chosen(askers[k], slot_of(order[k]), 1)]
        for c in range(chunks):
            send_right[k, c] = held[:, c * CHUNK : (c + 1) * CHUNK]
    for r, other in enumerate(others):
        offset = pick(share_of(other, me), order)
        held = acts[chosen(me, slot_of(offset), 0)]
        for c in range(chunks):
            send_left[r, c] = held[:, c * CHUNK : (c + 1) * CHUNK]
    my_rows = pl.ds(pl.multiple_of(dp * rows, rows), rows)
    held = acts[chosen(me, slot_of(my_offset), 0)]
    for c in range(chunks):
        left_rows[c, my_rows, :] = held[:, c * CHUNK : (c + 1) * CHUNK]

    def left_copy(r, c):
        return pltpu.make_async_remote_copy(
            src_ref=send_left.at[r, c],
            dst_ref=left_rows.at[c, my_rows, :],
            send_sem=left_send_sem.at[r, c],
            recv_sem=left_sem.at[c, dp],
            device_id=(others[r], me),
            device_id_type=MESH,
        )

    def right_copy(k, c):
        return pltpu.make_async_remote_copy(
            src_ref=send_right.at[k, c],
            dst_ref=right_rows.at[c, my_rows, :],
            send_sem=right_send_sem.at[k, c],
            recv_sem=right_sem.at[c, dp],
            device_id=(ask_member[k], askers[k]),
            device_id_type=MESH,
        )

    pl.semaphore_wait(barrier, len(greeted))
    ahead = (2 * chunks + 2) // 3
    for c in range(chunks):
        for k in range(groups):
            right_copy(k, c).start()
        if c < ahead:
            for at in range(c * chunks // ahead, (c + 1) * chunks // ahead):
                for r in range(groups - 1):
                    left_copy(r, at).start()

    best[...] = jnp.full_like(best, -jnp.inf)
    for i in range(chunks):
        at = slice(i * CHUNK, (i + 1) * CHUNK)
        for other in others:
            theirs = pl.ds(pl.multiple_of(other * rows, rows), rows)
            pltpu.make_async_remote_copy(
                src_ref=send_left.at[0, 0],
                dst_ref=left_rows.at[i, theirs, :],
                send_sem=left_send_sem.at[0, 0],
                recv_sem=left_sem.at[i, other],
                device_id=(other, me),
                device_id_type=MESH,
            ).wait_recv()
        block = left_rows[i]
        wide = block.astype(jnp.float32)
        square = jnp.sum(wide * wide, axis=0, keepdims=True) / all_rows
        inverse = 1.0 / jnp.sqrt(square + EPSILON)
        inv_left[at, :] = jnp.broadcast_to(inverse, (128, CHUNK)).T
        turned[at, :] = block.T

    @pl.loop(0, chunks)
    def _(c):
        for member in range(groups):
            pltpu.make_async_remote_copy(
                src_ref=send_right.at[0, 0],
                dst_ref=right_rows.at[c, pl.ds(member * rows, rows), :],
                send_sem=right_send_sem.at[0, 0],
                recv_sem=right_sem.at[c, member],
                device_id=(member, partner),
                device_id_type=MESH,
            ).wait_recv()
        block = right_rows[c]
        wide = block.astype(jnp.float32)
        square = jnp.sum(wide * wide, axis=0, keepdims=True) / all_rows
        inverse = 1.0 / jnp.sqrt(square + EPSILON)
        tops = [jnp.full((8, 128), -jnp.inf, jnp.float32) for _ in range(CHUNK // 128)]
        for i in range(chunks):
            at = slice(i * CHUNK, (i + 1) * CHUNK)
            gram = jnp.dot(turned[at, :], block, preferred_element_type=jnp.float32)
            scale = inv_left[at, :]
            running = best[at, :]
            for h in range(CHUNK // 128):
                lanes = slice(h * 128, (h + 1) * 128)
                scaled = gram[:, lanes] * scale
                running = jnp.maximum(running, scaled * inverse[:, lanes])
                gram_top = jnp.max(scaled.reshape(CHUNK // 8, 8, 128), axis=0)
                tops[h] = jnp.maximum(tops[h], gram_top)
            best[at, :] = running
        top = jnp.max(jnp.concatenate(tops, axis=1), axis=0, keepdims=True)
        right_row[c] = top * inverse / all_rows

    right_full = jnp.concatenate([right_row[c] for c in range(chunks)], axis=1)
    left_full = jnp.concatenate(
        [
            jnp.max(best[i * CHUNK : (i + 1) * CHUNK, :].T, axis=0, keepdims=True)
            for i in range(chunks)
        ],
        axis=1,
    ) / all_rows
    for member in range(groups):
        at = slice(member * part, (member + 1) * part)
        right_stage[member] = right_full[:, at]
        left_stage[member] = left_full[:, at]

    def right_result(member):
        return pltpu.make_async_remote_copy(
            src_ref=right_stage.at[member],
            dst_ref=right_got.at[mine],
            send_sem=out_send_sem.at[member],
            recv_sem=right_got_sem.at[mine],
            device_id=(member, partner),
            device_id_type=MESH,
        )

    def left_result(r):
        return pltpu.make_async_remote_copy(
            src_ref=left_stage.at[others[r]],
            dst_ref=left_got.at[mine],
            send_sem=out_send_sem.at[groups + r],
            recv_sem=left_got_sem.at[mine],
            device_id=(others[r], me),
            device_id_type=MESH,
        )

    for member in range(groups):
        right_result(member).start()
    for r in range(groups - 1):
        left_result(r).start()
    left_got[mine] = left_stage[dp]

    @pl.loop(0, chunks)
    def _(c):
        for r in range(groups - 1):
            left_copy(r, c).wait_send()
        for k in range(groups):
            right_copy(k, c).wait_send()

    for other in others:
        share = share_of(other, me)
        pltpu.make_async_remote_copy(
            src_ref=left_stage.at[0],
            dst_ref=left_got.at[share],
            send_sem=out_send_sem.at[0],
            recv_sem=left_got_sem.at[share],
            device_id=(other, me),
            device_id_type=MESH,
        ).wait_recv()
    for k in range(groups):
        pltpu.make_async_remote_copy(
            src_ref=right_stage.at[0],
            dst_ref=right_got.at[k],
            send_sem=out_send_sem.at[0],
            recv_sem=right_got_sem.at[k],
            device_id=(ask_member[k], askers[k]),
            device_id_type=MESH,
        ).wait_recv()
    for member in range(groups):
        right_result(member).wait_send()
    for r in range(groups - 1):
        left_result(r).wait_send()

    for s in range(groups):
        offset = pairs_ref[1, s] // per_device
        share = 0
        for k in range(groups):
            share = share + jnp.where(offset == order[k], k, 0)
        left_out[0, s : s + 1, :] = left_got[share]
        right_out[0, s : s + 1, :] = right_got[share]


def pair_call(order, turns, n, groups, collective_id, unit_codes, block_scales, pairs):
    per_device, rows, units = unit_codes.shape
    chunks = units // CHUNK
    part = units // groups
    out = jax.ShapeDtypeStruct((1, groups, part), jnp.float32)
    vmem = pl.BlockSpec(memory_space=pltpu.VMEM)
    dma = pltpu.SemaphoreType.DMA
    return pl.pallas_call(
        functools.partial(pair_kernel, order, turns, n, groups),
        out_shape=(out, out),
        in_specs=[vmem, vmem, pl.BlockSpec(memory_space=pltpu.SMEM)],
        out_specs=(vmem, vmem),
        scratch_shapes=[
            pltpu.VMEM((per_device, rows, units), jnp.bfloat16),
            pltpu.VMEM((groups - 1, chunks, rows, CHUNK), jnp.bfloat16),
            pltpu.VMEM((groups, chunks, rows, CHUNK), jnp.bfloat16),
            pltpu.VMEM((chunks, groups * rows, CHUNK), jnp.bfloat16),
            pltpu.VMEM((chunks, groups * rows, CHUNK), jnp.bfloat16),
            pltpu.VMEM((units, groups * rows), jnp.bfloat16),
            pltpu.VMEM((units, 128), jnp.float32),
            pltpu.VMEM((units, 128), jnp.float32),
            pltpu.VMEM((chunks, 1, CHUNK), jnp.float32),
            pltpu.VMEM((groups, 1, part), jnp.float32),
            pltpu.VMEM((groups, 1, part), jnp.float32),
            pltpu.VMEM((groups, 1, part), jnp.float32),
            pltpu.VMEM((groups, 1, part), jnp.float32),
            dma((groups - 1, chunks)),
            dma((chunks, groups)),
            dma((groups, chunks)),
            dma((chunks, groups)),
            dma((2 * groups - 1,)),
            dma((groups,)),
            dma((groups,)),
        ],
        compiler_params=pltpu.CompilerParams(
            collective_id=collective_id, has_side_effects=True, vmem_limit_bytes=24 * 2**20
        ),
        cost_estimate=pl.CostEstimate(
            flops=2 * units * units * groups * rows, bytes_accessed=2 * units * rows * per_device, transcendentals=0
        ),
    )(unit_codes, block_scales, pairs)


def offset_sets(n, slots):
    fixed = sorted({1, n // 2, n - 1})
    rest = [o for o in range(1, n) if o not in fixed]
    free = slots - len(fixed)
    if free < 0 or math.comb(len(rest), free) > MAX_BRANCHES:
        return []
    return [tuple(sorted(fixed + list(more))) for more in itertools.combinations(rest, free)]


def body(unit_codes, block_scales, pair_list):
    n = lax.axis_size("expert")
    groups = lax.axis_size("dp")
    per_device, rows, units = unit_codes.shape
    slots = pair_list.shape[0] // n
    sets = offset_sets(n, slots)
    fits = (
        slots == groups
        and rows % 16 == 0
        and units % CHUNK == 0
        and units % (128 * groups) == 0
        and (groups * rows) % 128 == 0
    )
    if not sets or not fits:
        return general_body(unit_codes, block_scales, pair_list)
    offsets = pair_list[:slots, 1] // per_device
    if slots == 4 and n > 4:
        free = [(sum(members) - 1 - n // 2 - (n - 1), at) for at, members in enumerate(sets)]
        branch = jnp.sum(sum(jnp.where(offsets == offset, at, 0) for offset, at in free))
    else:
        branch = 0
        for at, members in enumerate(sets):
            same = jnp.all(jnp.any(offsets[:, None] == jnp.asarray(members)[None, :], axis=1))
            branch = branch + jnp.where(same, at, 0)
    calls = []
    for at, members in enumerate(sets):
        order, turns = TURNS.get(members, (members, (0,) * n)) if (n, groups) == (8, 4) else (members, (0,) * n)
        calls.append(functools.partial(pair_call, order, turns, n, groups, at))
    return lax.switch(branch, calls, unit_codes, block_scales, pair_list.T)


def solution(mesh):
    in_specs = (P("expert", "dp", None), P("expert", None, "dp"), P())
    out_specs = (P("expert", None, "dp"), P("expert", None, "dp"))
    return jax.shard_map(body, mesh=mesh, in_specs=in_specs, out_specs=out_specs, check_vma=False)
```

```python
import functools
import itertools
import math

import jax
import jax.numpy as jnp
from jax import lax
from jax.experimental import pallas as pl
from jax.experimental.pallas import tpu as pltpu
from jax.sharding import PartitionSpec as P

EPSILON = 1e-06


def general_body(unit_codes, block_scales, pair_list):
    num_devices = lax.axis_size("expert")
    groups = lax.axis_size("dp")
    my_index = lax.axis_index("expert")
    dp_index = lax.axis_index("dp")
    per_device, row_count, unit_count = unit_codes.shape
    num_blocks = block_scales.shape[1]
    block_len = unit_count // num_blocks
    slice_width = unit_count // groups
    factor = jnp.transpose(block_scales, (0, 2, 1))[:, :, :, None]
    acts = (
        unit_codes.astype(jnp.float32).reshape(per_device, row_count, num_blocks, block_len)
        * factor
    )
    acts = acts.reshape(per_device, row_count, unit_count).astype(jnp.bfloat16)
    slot_count = pair_list.shape[0] // num_devices
    pair_table = pair_list.reshape(num_devices, slot_count, 2)
    my_pairs = lax.dynamic_index_in_dim(pair_table, my_index, 0, keepdims=False)
    left_local = my_pairs[:, 0] % per_device
    right_dev = my_pairs[:, 1] // per_device
    is_asked = pair_table[:, :, 1] // per_device == my_index
    chosen = jnp.sum(jnp.where(is_asked, pair_table[:, :, 1] % per_device, 0), axis=1)
    in_use = jnp.any(is_asked, axis=1)
    chooser = ((chosen[:, None] == jnp.arange(per_device)[None, :]) & in_use[:, None]).astype(
        jnp.bfloat16
    )
    own_full = lax.all_gather(acts, "dp", axis=1, tiled=True)
    flattened = acts.reshape(per_device, -1)
    outbound = jnp.dot(chooser, flattened, preferred_element_type=jnp.float32).astype(jnp.bfloat16)
    received = lax.all_to_all(
        outbound.reshape((num_devices,) + acts.shape[1:]),
        "expert",
        split_axis=0,
        concat_axis=0,
        tiled=True,
    )
    wanted = jnp.take(received, right_dev, axis=0)
    partner = lax.all_to_all(wanted, "dp", split_axis=2, concat_axis=1, tiled=True)
    all_rows = partner.shape[1]
    own_square = (
        jnp.einsum("era,era->ea", own_full, own_full, preferred_element_type=jnp.float32) / all_rows
    )
    inv_own = 1.0 / jnp.sqrt(own_square + EPSILON)
    part_square = (
        jnp.einsum("srb,srb->sb", partner, partner, preferred_element_type=jnp.float32) / all_rows
    )
    inv_part = 1.0 / jnp.sqrt(part_square + EPSILON)

    def single(member):
        expert_pick, partner_block, inv_unit = member
        left_rows = jnp.take(own_full, expert_pick, axis=0)
        gram_block = jnp.einsum(
            "ra,rb->ab", left_rows, partner_block, preferred_element_type=jnp.float32
        )
        correlation = (
            gram_block
            / all_rows
            * jnp.take(inv_own, expert_pick, axis=0)[:, None]
            * inv_unit[None, :]
        )
        return (jnp.max(correlation, axis=1), jnp.max(correlation, axis=0))

    def several(member):
        return jax.vmap(single)(member)

    bundle = math.gcd(slot_count, 4)
    stacked = (
        left_local.reshape(-1, bundle),
        partner.reshape(-1, bundle, all_rows, slice_width),
        inv_part.reshape(-1, bundle, slice_width),
    )
    left_part, right_part = lax.map(several, stacked)
    left_part = left_part.reshape(slot_count, unit_count)
    right_part = right_part.reshape(slot_count, slice_width)
    left_all = lax.pmax(left_part, "dp")
    left_out = lax.dynamic_slice_in_dim(left_all, dp_index * slice_width, slice_width, 1)
    target = (right_dev[:, None] == jnp.arange(num_devices)[None, :]).astype(jnp.float32)
    outgoing = jnp.dot(
        target.T, right_part, precision=lax.Precision.HIGHEST, preferred_element_type=jnp.float32
    )
    returned = lax.all_to_all(outgoing, "expert", split_axis=0, concat_axis=0, tiled=True)
    offsets = pair_table[0, :, 1] // per_device
    source_dev = (my_index - offsets) % num_devices
    right_out = jnp.take(returned, source_dev, axis=0)
    return (left_out[None], right_out[None])


MESH = pl.DeviceIdType.MESH
CHUNK = 256
MAX_BRANCHES = 8
TURNS = {
    (1, 2, 4, 7): ((1, 7, 4, 2), (1, 1, 2, 2, 0, 3, 1, 0)),
    (1, 3, 4, 7): ((1, 4, 7, 3), (0, 1, 3, 0, 3, 1, 2, 0)),
    (1, 4, 5, 7): ((1, 4, 7, 5), (0, 0, 1, 3, 3, 2, 1, 2)),
    (1, 4, 6, 7): ((1, 7, 6, 4), (0, 2, 1, 3, 2, 3, 3, 0)),
}


def pick(index, table):
    total = 0
    size = len(table)
    for at, value in enumerate(table):
        if value:
            apart = (index - at) * (index - at)
            total = total + value * (1 - (apart + size * size - 1) // (size * size))
    return total


def pair_kernel(
    order, turns, n, groups,
    codes_ref, scales_ref, pairs_ref, left_out, right_out,
    codes, acts, send_left, send_right, left_rows, right_rows, turned, inv_left, best, right_row,
    left_stage, right_stage, left_got, right_got,
    load_sem, left_send_sem, left_sem, right_send_sem, right_sem, out_send_sem, left_got_sem, right_got_sem,
):
    me = lax.axis_index("expert")
    dp = lax.axis_index("dp")
    per_device, rows, units = codes_ref.shape
    blocks = scales_ref.shape[0]
    width = units // blocks
    chunks = units // CHUNK
    part = units // groups
    all_rows = groups * rows

    def share_of(member, column):
        return (member - pick(column, turns) + groups) % groups

    def member_of(share, column):
        return (share + pick(column, turns)) % groups

    mine = share_of(dp, me)
    my_offset = pick(mine, order)
    partner = (me + my_offset) % n
    askers = [(me - order[k] + n) % n for k in range(groups)]
    ask_member = [member_of(k, askers[k]) for k in range(groups)]
    others = [(dp + r) % groups for r in range(1, groups)]

    barrier = pltpu.get_barrier_semaphore()
    greeted = [(other, me) for other in others]
    greeted += [(ask_member[k], askers[k]) for k in range(groups)]
    greeted += [(member, partner) for member in range(groups)]
    for device in greeted:
        pl.semaphore_signal(barrier, inc=1, device_id=device, device_id_type=MESH)

    load = pltpu.make_async_copy(codes_ref, codes, load_sem)
    load.start()

    def slot_of(offset):
        slot = 0
        for s in range(groups):
            slot = slot + jnp.where(pairs_ref[1, s] // per_device == offset, s, 0)
        return slot

    def chosen(column, slot, side):
        return lax.rem(pairs_ref[side, groups * column + slot], per_device)

    my_rows = pl.ds(pl.multiple_of(dp * rows, rows), rows)
    right_pick = [chosen(askers[k], slot_of(order[k]), 1) for k in range(groups)]
    left_pick = [
        chosen(me, slot_of(pick(share_of(member, me), order)), 0) for member in others + [dp]
    ]
    factors = [scales_ref[:, expert, :].T for expert in range(per_device)]

    def scale_and_stage(c):
        for expert in range(per_device):
            for block in range(c * CHUNK // width, (c + 1) * CHUNK // width):
                at = slice(block * width, (block + 1) * width)
                inside = slice(block * width - c * CHUNK, (block + 1) * width - c * CHUNK)
                acts[expert, c, :, inside] = (
                    codes[expert, :, at].astype(jnp.float32) * factors[expert][:, block : block + 1]
                ).astype(jnp.bfloat16)
        for k in range(groups):
            send_right[k, c] = acts[right_pick[k], c]
        for r in range(groups - 1):
            send_left[r, c] = acts[left_pick[r], c]
        left_rows[c, my_rows, :] = acts[left_pick[-1], c]

    def left_copy(r, c):
        return pltpu.make_async_remote_copy(
            src_ref=send_left.at[r, c],
            dst_ref=left_rows.at[c, my_rows, :],
            send_sem=left_send_sem.at[r, c],
            recv_sem=left_sem.at[c, dp],
            device_id=(others[r], me),
            device_id_type=MESH,
        )

    def right_copy(k, c):
        return pltpu.make_async_remote_copy(
            src_ref=send_right.at[k, c],
            dst_ref=right_rows.at[c, my_rows, :],
            send_sem=right_send_sem.at[k, c],
            recv_sem=right_sem.at[c, dp],
            device_id=(ask_member[k], askers[k]),
            device_id_type=MESH,
        )

    load.wait()
    ahead = (2 * chunks + 2) // 3
    staged = 0
    for c in range(chunks):
        lefts = range(c * chunks // ahead, (c + 1) * chunks // ahead) if c < ahead else range(0)
        while staged <= max([c, *lefts]):
            scale_and_stage(staged)
            staged += 1
        if c == 0:
            pl.semaphore_wait(barrier, len(greeted))
        for k in range(groups):
            right_copy(k, c).start()
        for at in lefts:
            for r in range(groups - 1):
                left_copy(r, at).start()

    best[...] = jnp.full_like(best, -jnp.inf)
    for i in range(chunks):
        at = slice(i * CHUNK, (i + 1) * CHUNK)
        for other in others:
            theirs = pl.ds(pl.multiple_of(other * rows, rows), rows)
            pltpu.make_async_remote_copy(
                src_ref=send_left.at[0, 0],
                dst_ref=left_rows.at[i, theirs, :],
                send_sem=left_send_sem.at[0, 0],
                recv_sem=left_sem.at[i, other],
                device_id=(other, me),
                device_id_type=MESH,
            ).wait_recv()
        block = left_rows[i]
        wide = block.astype(jnp.float32)
        square = jnp.sum(wide * wide, axis=0, keepdims=True) / all_rows
        inverse = 1.0 / jnp.sqrt(square + EPSILON)
        inv_left[at, :] = jnp.broadcast_to(inverse, (128, CHUNK)).T
        turned[at, :] = block.T

    @pl.loop(0, chunks)
    def _(c):
        for member in range(groups):
            pltpu.make_async_remote_copy(
                src_ref=send_right.at[0, 0],
                dst_ref=right_rows.at[c, pl.ds(member * rows, rows), :],
                send_sem=right_send_sem.at[0, 0],
                recv_sem=right_sem.at[c, member],
                device_id=(member, partner),
                device_id_type=MESH,
            ).wait_recv()
        block = right_rows[c]
        wide = block.astype(jnp.float32)
        square = jnp.sum(wide * wide, axis=0, keepdims=True) / all_rows
        inverse = 1.0 / jnp.sqrt(square + EPSILON)
        tops = [jnp.full((8, 128), -jnp.inf, jnp.float32) for _ in range(CHUNK // 128)]
        for i in range(chunks):
            at = slice(i * CHUNK, (i + 1) * CHUNK)
            gram = jnp.dot(turned[at, :], block, preferred_element_type=jnp.float32)
            scale = inv_left[at, :]
            running = best[at, :]
            for h in range(CHUNK // 128):
                lanes = slice(h * 128, (h + 1) * 128)
                scaled = gram[:, lanes] * scale
                running = jnp.maximum(running, scaled * inverse[:, lanes])
                gram_top = jnp.max(scaled.reshape(CHUNK // 8, 8, 128), axis=0)
                tops[h] = jnp.maximum(tops[h], gram_top)
            best[at, :] = running
        top = jnp.max(jnp.concatenate(tops, axis=1), axis=0, keepdims=True)
        right_row[c] = top * inverse / all_rows

    right_full = jnp.concatenate([right_row[c] for c in range(chunks)], axis=1)
    left_full = jnp.concatenate(
        [
            jnp.max(best[i * CHUNK : (i + 1) * CHUNK, :].T, axis=0, keepdims=True)
            for i in range(chunks)
        ],
        axis=1,
    ) / all_rows
    for member in range(groups):
        at = slice(member * part, (member + 1) * part)
        right_stage[member] = right_full[:, at]
        left_stage[member] = left_full[:, at]

    def right_result(member):
        return pltpu.make_async_remote_copy(
            src_ref=right_stage.at[member],
            dst_ref=right_got.at[mine],
            send_sem=out_send_sem.at[member],
            recv_sem=right_got_sem.at[mine],
            device_id=(member, partner),
            device_id_type=MESH,
        )

    def left_result(r):
        return pltpu.make_async_remote_copy(
            src_ref=left_stage.at[others[r]],
            dst_ref=left_got.at[mine],
            send_sem=out_send_sem.at[groups + r],
            recv_sem=left_got_sem.at[mine],
            device_id=(others[r], me),
            device_id_type=MESH,
        )

    for member in range(groups):
        right_result(member).start()
    for r in range(groups - 1):
        left_result(r).start()
    left_got[mine] = left_stage[dp]

    @pl.loop(0, chunks)
    def _(c):
        for r in range(groups - 1):
            left_copy(r, c).wait_send()
        for k in range(groups):
            right_copy(k, c).wait_send()

    for other in others:
        share = share_of(other, me)
        pltpu.make_async_remote_copy(
            src_ref=left_stage.at[0],
            dst_ref=left_got.at[share],
            send_sem=out_send_sem.at[0],
            recv_sem=left_got_sem.at[share],
            device_id=(other, me),
            device_id_type=MESH,
        ).wait_recv()
    for k in range(groups):
        pltpu.make_async_remote_copy(
            src_ref=right_stage.at[0],
            dst_ref=right_got.at[k],
            send_sem=out_send_sem.at[0],
            recv_sem=right_got_sem.at[k],
            device_id=(ask_member[k], askers[k]),
            device_id_type=MESH,
        ).wait_recv()
    for member in range(groups):
        right_result(member).wait_send()
    for r in range(groups - 1):
        left_result(r).wait_send()

    for s in range(groups):
        offset = pairs_ref[1, s] // per_device
        share = 0
        for k in range(groups):
            share = share + jnp.where(offset == order[k], k, 0)
        left_out[0, s : s + 1, :] = left_got[share]
        right_out[0, s : s + 1, :] = right_got[share]


def pair_call(order, turns, n, groups, collective_id, unit_codes, block_scales, pairs):
    per_device, rows, units = unit_codes.shape
    chunks = units // CHUNK
    part = units // groups
    out = jax.ShapeDtypeStruct((1, groups, part), jnp.float32)
    vmem = pl.BlockSpec(memory_space=pltpu.VMEM)
    dma = pltpu.SemaphoreType.DMA
    return pl.pallas_call(
        functools.partial(pair_kernel, order, turns, n, groups),
        out_shape=(out, out),
        in_specs=[pl.BlockSpec(memory_space=pl.ANY), vmem, pl.BlockSpec(memory_space=pltpu.SMEM)],
        out_specs=(vmem, vmem),
        scratch_shapes=[
            pltpu.VMEM((per_device, rows, units), jnp.bfloat16),
            pltpu.VMEM((per_device, chunks, rows, CHUNK), jnp.bfloat16),
            pltpu.VMEM((groups - 1, chunks, rows, CHUNK), jnp.bfloat16),
            pltpu.VMEM((groups, chunks, rows, CHUNK), jnp.bfloat16),
            pltpu.VMEM((chunks, groups * rows, CHUNK), jnp.bfloat16),
            pltpu.VMEM((chunks, groups * rows, CHUNK), jnp.bfloat16),
            pltpu.VMEM((units, groups * rows), jnp.bfloat16),
            pltpu.VMEM((units, 128), jnp.float32),
            pltpu.VMEM((units, 128), jnp.float32),
            pltpu.VMEM((chunks, 1, CHUNK), jnp.float32),
            pltpu.VMEM((groups, 1, part), jnp.float32),
            pltpu.VMEM((groups, 1, part), jnp.float32),
            pltpu.VMEM((groups, 1, part), jnp.float32),
            pltpu.VMEM((groups, 1, part), jnp.float32),
            dma,
            dma((groups - 1, chunks)),
            dma((chunks, groups)),
            dma((groups, chunks)),
            dma((chunks, groups)),
            dma((2 * groups - 1,)),
            dma((groups,)),
            dma((groups,)),
        ],
        compiler_params=pltpu.CompilerParams(
            collective_id=collective_id, has_side_effects=True, vmem_limit_bytes=56 * 2**20
        ),
        cost_estimate=pl.CostEstimate(
            flops=2 * units * units * groups * rows, bytes_accessed=2 * units * rows * per_device, transcendentals=0
        ),
    )(unit_codes, jnp.transpose(block_scales, (1, 0, 2)), pairs)


def offset_sets(n, slots):
    fixed = sorted({1, n // 2, n - 1})
    rest = [o for o in range(1, n) if o not in fixed]
    free = slots - len(fixed)
    if free < 0 or math.comb(len(rest), free) > MAX_BRANCHES:
        return []
    return [tuple(sorted(fixed + list(more))) for more in itertools.combinations(rest, free)]


def body(unit_codes, block_scales, pair_list):
    n = lax.axis_size("expert")
    groups = lax.axis_size("dp")
    per_device, rows, units = unit_codes.shape
    slots = pair_list.shape[0] // n
    sets = offset_sets(n, slots)
    fits = (
        slots == groups
        and rows % 16 == 0
        and units % CHUNK == 0
        and CHUNK % (units // block_scales.shape[1]) == 0
        and units // block_scales.shape[1] % 128 == 0
        and units % (128 * groups) == 0
        and (groups * rows) % 128 == 0
    )
    if not sets or not fits:
        return general_body(unit_codes, block_scales, pair_list)
    offsets = pair_list[:slots, 1] // per_device
    if slots == 4 and n > 4:
        free = [(sum(members) - 1 - n // 2 - (n - 1), at) for at, members in enumerate(sets)]
        branch = jnp.sum(sum(jnp.where(offsets == offset, at, 0) for offset, at in free))
    else:
        branch = 0
        for at, members in enumerate(sets):
            same = jnp.all(jnp.any(offsets[:, None] == jnp.asarray(members)[None, :], axis=1))
            branch = branch + jnp.where(same, at, 0)
    calls = []
    for at, members in enumerate(sets):
        order, turns = TURNS.get(members, (members, (0,) * n)) if (n, groups) == (8, 4) else (members, (0,) * n)
        calls.append(functools.partial(pair_call, order, turns, n, groups, at))
    return lax.switch(branch, calls, unit_codes, block_scales, pair_list.T)


def solution(mesh):
    in_specs = (P("expert", "dp", None), P("expert", None, "dp"), P())
    out_specs = (P("expert", None, "dp"), P("expert", None, "dp"))
    return jax.shard_map(body, mesh=mesh, in_specs=in_specs, out_specs=out_specs, check_vma=False)
```

```python
import functools
import itertools
import math

import jax
import jax.numpy as jnp
from jax import lax
from jax.experimental import pallas as pl
from jax.experimental.pallas import tpu as pltpu
from jax.sharding import PartitionSpec as P

EPSILON = 1e-06


def general_body(unit_codes, block_scales, pair_list):
    num_devices = lax.axis_size("expert")
    groups = lax.axis_size("dp")
    my_index = lax.axis_index("expert")
    dp_index = lax.axis_index("dp")
    per_device, row_count, unit_count = unit_codes.shape
    num_blocks = block_scales.shape[1]
    block_len = unit_count // num_blocks
    slice_width = unit_count // groups
    factor = jnp.transpose(block_scales, (0, 2, 1))[:, :, :, None]
    acts = (
        unit_codes.astype(jnp.float32).reshape(per_device, row_count, num_blocks, block_len)
        * factor
    )
    acts = acts.reshape(per_device, row_count, unit_count).astype(jnp.bfloat16)
    slot_count = pair_list.shape[0] // num_devices
    pair_table = pair_list.reshape(num_devices, slot_count, 2)
    my_pairs = lax.dynamic_index_in_dim(pair_table, my_index, 0, keepdims=False)
    left_local = my_pairs[:, 0] % per_device
    right_dev = my_pairs[:, 1] // per_device
    is_asked = pair_table[:, :, 1] // per_device == my_index
    chosen = jnp.sum(jnp.where(is_asked, pair_table[:, :, 1] % per_device, 0), axis=1)
    in_use = jnp.any(is_asked, axis=1)
    chooser = ((chosen[:, None] == jnp.arange(per_device)[None, :]) & in_use[:, None]).astype(
        jnp.bfloat16
    )
    own_full = lax.all_gather(acts, "dp", axis=1, tiled=True)
    flattened = acts.reshape(per_device, -1)
    outbound = jnp.dot(chooser, flattened, preferred_element_type=jnp.float32).astype(jnp.bfloat16)
    received = lax.all_to_all(
        outbound.reshape((num_devices,) + acts.shape[1:]),
        "expert",
        split_axis=0,
        concat_axis=0,
        tiled=True,
    )
    wanted = jnp.take(received, right_dev, axis=0)
    partner = lax.all_to_all(wanted, "dp", split_axis=2, concat_axis=1, tiled=True)
    all_rows = partner.shape[1]
    own_square = (
        jnp.einsum("era,era->ea", own_full, own_full, preferred_element_type=jnp.float32) / all_rows
    )
    inv_own = 1.0 / jnp.sqrt(own_square + EPSILON)
    part_square = (
        jnp.einsum("srb,srb->sb", partner, partner, preferred_element_type=jnp.float32) / all_rows
    )
    inv_part = 1.0 / jnp.sqrt(part_square + EPSILON)

    def single(member):
        expert_pick, partner_block, inv_unit = member
        left_rows = jnp.take(own_full, expert_pick, axis=0)
        gram_block = jnp.einsum(
            "ra,rb->ab", left_rows, partner_block, preferred_element_type=jnp.float32
        )
        correlation = (
            gram_block
            / all_rows
            * jnp.take(inv_own, expert_pick, axis=0)[:, None]
            * inv_unit[None, :]
        )
        return (jnp.max(correlation, axis=1), jnp.max(correlation, axis=0))

    def several(member):
        return jax.vmap(single)(member)

    bundle = math.gcd(slot_count, 4)
    stacked = (
        left_local.reshape(-1, bundle),
        partner.reshape(-1, bundle, all_rows, slice_width),
        inv_part.reshape(-1, bundle, slice_width),
    )
    left_part, right_part = lax.map(several, stacked)
    left_part = left_part.reshape(slot_count, unit_count)
    right_part = right_part.reshape(slot_count, slice_width)
    left_all = lax.pmax(left_part, "dp")
    left_out = lax.dynamic_slice_in_dim(left_all, dp_index * slice_width, slice_width, 1)
    target = (right_dev[:, None] == jnp.arange(num_devices)[None, :]).astype(jnp.float32)
    outgoing = jnp.dot(
        target.T, right_part, precision=lax.Precision.HIGHEST, preferred_element_type=jnp.float32
    )
    returned = lax.all_to_all(outgoing, "expert", split_axis=0, concat_axis=0, tiled=True)
    offsets = pair_table[0, :, 1] // per_device
    source_dev = (my_index - offsets) % num_devices
    right_out = jnp.take(returned, source_dev, axis=0)
    return (left_out[None], right_out[None])


MESH = pl.DeviceIdType.MESH
CHUNK = 256
MAX_BRANCHES = 8
TURNS = {
    (1, 2, 4, 7): ((1, 7, 4, 2), (1, 1, 2, 2, 0, 3, 1, 0)),
    (1, 3, 4, 7): ((1, 4, 7, 3), (0, 1, 3, 0, 3, 1, 2, 0)),
    (1, 4, 5, 7): ((1, 4, 7, 5), (0, 0, 1, 3, 3, 2, 1, 2)),
    (1, 4, 6, 7): ((1, 7, 6, 4), (0, 2, 1, 3, 2, 3, 3, 0)),
}


def pick(index, table):
    total = 0
    size = len(table)
    for at, value in enumerate(table):
        if value:
            apart = (index - at) * (index - at)
            total = total + value * (1 - (apart + size * size - 1) // (size * size))
    return total


def pair_kernel(
    order, turns, n, groups,
    codes_ref, scales_ref, pairs_ref, out_ref,
    codes, acts, send_left, send_right, left_rows, right_rows, turned, inv_left, best, right_row,
    left_stage, right_stage, left_got, right_got,
    load_sem, left_send_sem, left_sem, right_send_sem, right_sem, out_send_sem, left_got_sem, right_got_sem,
):
    me = lax.axis_index("expert")
    dp = lax.axis_index("dp")
    per_device, rows, units = codes_ref.shape
    blocks = scales_ref.shape[0]
    width = units // blocks
    chunks = units // CHUNK
    part = units // groups
    all_rows = groups * rows

    def share_of(member, column):
        return (member - pick(column, turns) + groups) % groups

    def member_of(share, column):
        return (share + pick(column, turns)) % groups

    mine = share_of(dp, me)
    my_offset = pick(mine, order)
    partner = (me + my_offset) % n
    askers = [(me - order[k] + n) % n for k in range(groups)]
    ask_member = [member_of(k, askers[k]) for k in range(groups)]
    others = [(dp + r) % groups for r in range(1, groups)]

    barrier = pltpu.get_barrier_semaphore()
    greeted = [(other, me) for other in others]
    greeted += [(ask_member[k], askers[k]) for k in range(groups)]
    greeted += [(member, partner) for member in range(groups)]
    for device in greeted:
        pl.semaphore_signal(barrier, inc=1, device_id=device, device_id_type=MESH)

    load = pltpu.make_async_copy(codes_ref, codes, load_sem)
    load.start()

    def slot_of(offset):
        slot = 0
        for s in range(groups):
            slot = slot + jnp.where(pairs_ref[1, s] // per_device == offset, s, 0)
        return slot

    def chosen(column, slot, side):
        return lax.rem(pairs_ref[side, groups * column + slot], per_device)

    my_rows = pl.ds(pl.multiple_of(dp * rows, rows), rows)
    right_pick = [chosen(askers[k], slot_of(order[k]), 1) for k in range(groups)]
    left_pick = [
        chosen(me, slot_of(pick(share_of(member, me), order)), 0) for member in others + [dp]
    ]
    factors = [scales_ref[:, expert, :].T for expert in range(per_device)]

    def scale_and_stage(c):
        for expert in range(per_device):
            for block in range(c * CHUNK // width, (c + 1) * CHUNK // width):
                at = slice(block * width, (block + 1) * width)
                inside = slice(block * width - c * CHUNK, (block + 1) * width - c * CHUNK)
                acts[expert, c, :, inside] = (
                    codes[expert, :, at].astype(jnp.float32) * factors[expert][:, block : block + 1]
                ).astype(jnp.bfloat16)
        for k in range(groups):
            send_right[k, c] = acts[right_pick[k], c]
        for r in range(groups - 1):
            send_left[r, c] = acts[left_pick[r], c]
        left_rows[c, my_rows, :] = acts[left_pick[-1], c]

    def left_copy(r, c):
        return pltpu.make_async_remote_copy(
            src_ref=send_left.at[r, c],
            dst_ref=left_rows.at[c, my_rows, :],
            send_sem=left_send_sem.at[r, c],
            recv_sem=left_sem.at[c, dp],
            device_id=(others[r], me),
            device_id_type=MESH,
        )

    def right_copy(k, c):
        return pltpu.make_async_remote_copy(
            src_ref=send_right.at[k, c],
            dst_ref=right_rows.at[c, my_rows, :],
            send_sem=right_send_sem.at[k, c],
            recv_sem=right_sem.at[c, dp],
            device_id=(ask_member[k], askers[k]),
            device_id_type=MESH,
        )

    load.wait()
    ahead = (2 * chunks + 2) // 3
    staged = 0
    for c in range(chunks):
        lefts = range(c * chunks // ahead, (c + 1) * chunks // ahead) if c < ahead else range(0)
        while staged <= max([c, *lefts]):
            scale_and_stage(staged)
            staged += 1
        if c == 0:
            pl.semaphore_wait(barrier, len(greeted))
        for k in range(groups):
            right_copy(k, c).start()
        for at in lefts:
            for r in range(groups - 1):
                left_copy(r, at).start()

    best[...] = jnp.full_like(best, -jnp.inf)
    for i in range(chunks):
        at = slice(i * CHUNK, (i + 1) * CHUNK)
        for other in others:
            theirs = pl.ds(pl.multiple_of(other * rows, rows), rows)
            pltpu.make_async_remote_copy(
                src_ref=send_left.at[0, 0],
                dst_ref=left_rows.at[i, theirs, :],
                send_sem=left_send_sem.at[0, 0],
                recv_sem=left_sem.at[i, other],
                device_id=(other, me),
                device_id_type=MESH,
            ).wait_recv()
        block = left_rows[i]
        wide = block.astype(jnp.float32)
        square = jnp.sum(wide * wide, axis=0, keepdims=True) / all_rows
        inverse = 1.0 / jnp.sqrt(square + EPSILON)
        inv_left[at, :] = jnp.broadcast_to(inverse, (128, CHUNK)).T
        turned[at, :] = block.T

    @pl.loop(0, chunks)
    def _(c):
        for member in range(groups):
            pltpu.make_async_remote_copy(
                src_ref=send_right.at[0, 0],
                dst_ref=right_rows.at[c, pl.ds(member * rows, rows), :],
                send_sem=right_send_sem.at[0, 0],
                recv_sem=right_sem.at[c, member],
                device_id=(member, partner),
                device_id_type=MESH,
            ).wait_recv()
        block = right_rows[c]
        wide = block.astype(jnp.float32)
        square = jnp.sum(wide * wide, axis=0, keepdims=True) / all_rows
        inverse = 1.0 / jnp.sqrt(square + EPSILON)
        tops = [jnp.full((8, 128), -jnp.inf, jnp.float32) for _ in range(CHUNK // 128)]
        for i in range(chunks):
            at = slice(i * CHUNK, (i + 1) * CHUNK)
            gram = jnp.dot(turned[at, :], block, preferred_element_type=jnp.float32)
            scale = inv_left[at, :]
            running = best[at, :]
            for h in range(CHUNK // 128):
                lanes = slice(h * 128, (h + 1) * 128)
                scaled = gram[:, lanes] * scale
                running = jnp.maximum(running, scaled * inverse[:, lanes])
                gram_top = jnp.max(scaled.reshape(CHUNK // 8, 8, 128), axis=0)
                tops[h] = jnp.maximum(tops[h], gram_top)
            best[at, :] = running
        top = jnp.max(jnp.concatenate(tops, axis=1), axis=0, keepdims=True)
        right_row[c] = top * inverse / all_rows

    right_full = jnp.concatenate([right_row[c] for c in range(chunks)], axis=1)
    left_full = jnp.concatenate(
        [
            jnp.max(best[i * CHUNK : (i + 1) * CHUNK, :].T, axis=0, keepdims=True)
            for i in range(chunks)
        ],
        axis=1,
    ) / all_rows
    for member in range(groups):
        at = slice(member * part, (member + 1) * part)
        right_stage[member] = right_full[:, at]
        left_stage[member] = left_full[:, at]

    def right_result(member):
        return pltpu.make_async_remote_copy(
            src_ref=right_stage.at[member],
            dst_ref=right_got.at[mine],
            send_sem=out_send_sem.at[member],
            recv_sem=right_got_sem.at[mine],
            device_id=(member, partner),
            device_id_type=MESH,
        )

    def left_result(r):
        return pltpu.make_async_remote_copy(
            src_ref=left_stage.at[others[r]],
            dst_ref=left_got.at[mine],
            send_sem=out_send_sem.at[groups + r],
            recv_sem=left_got_sem.at[mine],
            device_id=(others[r], me),
            device_id_type=MESH,
        )

    for member in range(groups):
        right_result(member).start()
    for r in range(groups - 1):
        left_result(r).start()
    left_got[mine] = left_stage[dp]

    @pl.loop(0, chunks)
    def _(c):
        for r in range(groups - 1):
            left_copy(r, c).wait_send()
        for k in range(groups):
            right_copy(k, c).wait_send()

    for other in others:
        share = share_of(other, me)
        pltpu.make_async_remote_copy(
            src_ref=left_stage.at[0],
            dst_ref=left_got.at[share],
            send_sem=out_send_sem.at[0],
            recv_sem=left_got_sem.at[share],
            device_id=(other, me),
            device_id_type=MESH,
        ).wait_recv()
    for k in range(groups):
        pltpu.make_async_remote_copy(
            src_ref=right_stage.at[0],
            dst_ref=right_got.at[k],
            send_sem=out_send_sem.at[0],
            recv_sem=right_got_sem.at[k],
            device_id=(ask_member[k], askers[k]),
            device_id_type=MESH,
        ).wait_recv()
    for member in range(groups):
        right_result(member).wait_send()
    for r in range(groups - 1):
        left_result(r).wait_send()

    for s in range(groups):
        offset = pairs_ref[1, s] // per_device
        share = 0
        for k in range(groups):
            share = share + jnp.where(offset == order[k], k, 0)
        out_ref[s : s + 1, :] = left_got[share]
        out_ref[groups + s : groups + s + 1, :] = right_got[share]


def pair_call(order, turns, n, groups, collective_id, unit_codes, block_scales, pairs):
    per_device, rows, units = unit_codes.shape
    chunks = units // CHUNK
    part = units // groups
    out = jax.ShapeDtypeStruct((2 * groups, part), jnp.float32)
    vmem = pl.BlockSpec(memory_space=pltpu.VMEM)
    dma = pltpu.SemaphoreType.DMA
    return pl.pallas_call(
        functools.partial(pair_kernel, order, turns, n, groups),
        out_shape=out,
        in_specs=[pl.BlockSpec(memory_space=pl.ANY), vmem, pl.BlockSpec(memory_space=pltpu.SMEM)],
        out_specs=vmem,
        scratch_shapes=[
            pltpu.VMEM((per_device, rows, units), jnp.bfloat16),
            pltpu.VMEM((per_device, chunks, rows, CHUNK), jnp.bfloat16),
            pltpu.VMEM((groups - 1, chunks, rows, CHUNK), jnp.bfloat16),
            pltpu.VMEM((groups, chunks, rows, CHUNK), jnp.bfloat16),
            pltpu.VMEM((chunks, groups * rows, CHUNK), jnp.bfloat16),
            pltpu.VMEM((chunks, groups * rows, CHUNK), jnp.bfloat16),
            pltpu.VMEM((units, groups * rows), jnp.bfloat16),
            pltpu.VMEM((units, 128), jnp.float32),
            pltpu.VMEM((units, 128), jnp.float32),
            pltpu.VMEM((chunks, 1, CHUNK), jnp.float32),
            pltpu.VMEM((groups, 1, part), jnp.float32),
            pltpu.VMEM((groups, 1, part), jnp.float32),
            pltpu.VMEM((groups, 1, part), jnp.float32),
            pltpu.VMEM((groups, 1, part), jnp.float32),
            dma,
            dma((groups - 1, chunks)),
            dma((chunks, groups)),
            dma((groups, chunks)),
            dma((chunks, groups)),
            dma((2 * groups - 1,)),
            dma((groups,)),
            dma((groups,)),
        ],
        compiler_params=pltpu.CompilerParams(
            collective_id=collective_id, has_side_effects=True, vmem_limit_bytes=56 * 2**20
        ),
        cost_estimate=pl.CostEstimate(
            flops=2 * units * units * groups * rows, bytes_accessed=2 * units * rows * per_device, transcendentals=0
        ),
    )(unit_codes, jnp.transpose(block_scales, (1, 0, 2)), pairs)


def offset_sets(n, slots):
    fixed = sorted({1, n // 2, n - 1})
    rest = [o for o in range(1, n) if o not in fixed]
    free = slots - len(fixed)
    if free < 0 or math.comb(len(rest), free) > MAX_BRANCHES:
        return []
    return [tuple(sorted(fixed + list(more))) for more in itertools.combinations(rest, free)]


def body(unit_codes, block_scales, pair_list):
    n = lax.axis_size("expert")
    groups = lax.axis_size("dp")
    per_device, rows, units = unit_codes.shape
    slots = pair_list.shape[0] // n
    sets = offset_sets(n, slots)
    fits = (
        slots == groups
        and rows % 16 == 0
        and units % CHUNK == 0
        and CHUNK % (units // block_scales.shape[1]) == 0
        and units // block_scales.shape[1] % 128 == 0
        and units % (128 * groups) == 0
        and (groups * rows) % 128 == 0
    )
    if not sets or not fits:
        return general_body(unit_codes, block_scales, pair_list)
    offsets = pair_list[:slots, 1] // per_device
    if slots == 4 and n > 4:
        free = [(sum(members) - 1 - n // 2 - (n - 1), at) for at, members in enumerate(sets)]
        branch = jnp.sum(sum(jnp.where(offsets == offset, at, 0) for offset, at in free))
    else:
        branch = 0
        for at, members in enumerate(sets):
            same = jnp.all(jnp.any(offsets[:, None] == jnp.asarray(members)[None, :], axis=1))
            branch = branch + jnp.where(same, at, 0)
    calls = []
    for at, members in enumerate(sets):
        order, turns = TURNS.get(members, (members, (0,) * n)) if (n, groups) == (8, 4) else (members, (0,) * n)
        calls.append(functools.partial(pair_call, order, turns, n, groups, at))
    best = lax.switch(branch, calls, unit_codes, block_scales, pair_list.T)
    return (best[None, :slots], best[None, slots:])


def solution(mesh):
    in_specs = (P("expert", "dp", None), P("expert", None, "dp"), P())
    out_specs = (P("expert", None, "dp"), P("expert", None, "dp"))
    return jax.shard_map(body, mesh=mesh, in_specs=in_specs, out_specs=out_specs, check_vma=False)
```

```python
import functools
import itertools
import math

import jax
import jax.numpy as jnp
from jax import lax
from jax.experimental import pallas as pl
from jax.experimental.pallas import tpu as pltpu
from jax.sharding import PartitionSpec as P

EPSILON = 1e-06


def general_body(unit_codes, block_scales, pair_list):
    num_devices = lax.axis_size("expert")
    groups = lax.axis_size("dp")
    my_index = lax.axis_index("expert")
    dp_index = lax.axis_index("dp")
    per_device, row_count, unit_count = unit_codes.shape
    num_blocks = block_scales.shape[1]
    block_len = unit_count // num_blocks
    slice_width = unit_count // groups
    factor = jnp.transpose(block_scales, (0, 2, 1))[:, :, :, None]
    acts = (
        unit_codes.astype(jnp.float32).reshape(per_device, row_count, num_blocks, block_len)
        * factor
    )
    acts = acts.reshape(per_device, row_count, unit_count).astype(jnp.bfloat16)
    slot_count = pair_list.shape[0] // num_devices
    pair_table = pair_list.reshape(num_devices, slot_count, 2)
    my_pairs = lax.dynamic_index_in_dim(pair_table, my_index, 0, keepdims=False)
    left_local = my_pairs[:, 0] % per_device
    right_dev = my_pairs[:, 1] // per_device
    is_asked = pair_table[:, :, 1] // per_device == my_index
    chosen = jnp.sum(jnp.where(is_asked, pair_table[:, :, 1] % per_device, 0), axis=1)
    in_use = jnp.any(is_asked, axis=1)
    chooser = ((chosen[:, None] == jnp.arange(per_device)[None, :]) & in_use[:, None]).astype(
        jnp.bfloat16
    )
    own_full = lax.all_gather(acts, "dp", axis=1, tiled=True)
    flattened = acts.reshape(per_device, -1)
    outbound = jnp.dot(chooser, flattened, preferred_element_type=jnp.float32).astype(jnp.bfloat16)
    received = lax.all_to_all(
        outbound.reshape((num_devices,) + acts.shape[1:]),
        "expert",
        split_axis=0,
        concat_axis=0,
        tiled=True,
    )
    wanted = jnp.take(received, right_dev, axis=0)
    partner = lax.all_to_all(wanted, "dp", split_axis=2, concat_axis=1, tiled=True)
    all_rows = partner.shape[1]
    own_square = (
        jnp.einsum("era,era->ea", own_full, own_full, preferred_element_type=jnp.float32) / all_rows
    )
    inv_own = 1.0 / jnp.sqrt(own_square + EPSILON)
    part_square = (
        jnp.einsum("srb,srb->sb", partner, partner, preferred_element_type=jnp.float32) / all_rows
    )
    inv_part = 1.0 / jnp.sqrt(part_square + EPSILON)

    def single(member):
        expert_pick, partner_block, inv_unit = member
        left_rows = jnp.take(own_full, expert_pick, axis=0)
        gram_block = jnp.einsum(
            "ra,rb->ab", left_rows, partner_block, preferred_element_type=jnp.float32
        )
        correlation = (
            gram_block
            / all_rows
            * jnp.take(inv_own, expert_pick, axis=0)[:, None]
            * inv_unit[None, :]
        )
        return (jnp.max(correlation, axis=1), jnp.max(correlation, axis=0))

    def several(member):
        return jax.vmap(single)(member)

    bundle = math.gcd(slot_count, 4)
    stacked = (
        left_local.reshape(-1, bundle),
        partner.reshape(-1, bundle, all_rows, slice_width),
        inv_part.reshape(-1, bundle, slice_width),
    )
    left_part, right_part = lax.map(several, stacked)
    left_part = left_part.reshape(slot_count, unit_count)
    right_part = right_part.reshape(slot_count, slice_width)
    left_all = lax.pmax(left_part, "dp")
    left_out = lax.dynamic_slice_in_dim(left_all, dp_index * slice_width, slice_width, 1)
    target = (right_dev[:, None] == jnp.arange(num_devices)[None, :]).astype(jnp.float32)
    outgoing = jnp.dot(
        target.T, right_part, precision=lax.Precision.HIGHEST, preferred_element_type=jnp.float32
    )
    returned = lax.all_to_all(outgoing, "expert", split_axis=0, concat_axis=0, tiled=True)
    offsets = pair_table[0, :, 1] // per_device
    source_dev = (my_index - offsets) % num_devices
    right_out = jnp.take(returned, source_dev, axis=0)
    return (left_out[None], right_out[None])


MESH = pl.DeviceIdType.MESH
CHUNK = 256
MAX_BRANCHES = 8
TURNS = {
    (1, 2, 4, 7): ((1, 7, 4, 2), (1, 1, 2, 2, 0, 3, 1, 0)),
    (1, 3, 4, 7): ((1, 4, 7, 3), (0, 1, 3, 0, 3, 1, 2, 0)),
    (1, 4, 5, 7): ((1, 4, 7, 5), (0, 0, 1, 3, 3, 2, 1, 2)),
    (1, 4, 6, 7): ((1, 7, 6, 4), (0, 2, 1, 3, 2, 3, 3, 0)),
}


def pick(index, table):
    total = 0
    size = len(table)
    for at, value in enumerate(table):
        if value:
            apart = (index - at) * (index - at)
            total = total + value * (1 - (apart + size * size - 1) // (size * size))
    return total


def pair_kernel(
    order, turns, n, groups,
    codes_ref, scales_ref, pairs_ref, out_ref,
    codes, acts, send_left, send_right, left_rows, right_rows, turned, inv_left, best, right_row,
    left_stage, right_stage, left_got, right_got,
    load_sem, left_send_sem, left_sem, right_send_sem, right_sem, out_send_sem, left_got_sem, right_got_sem,
):
    me = lax.axis_index("expert")
    dp = lax.axis_index("dp")
    per_device, rows, units = codes_ref.shape
    blocks = scales_ref.shape[0]
    width = units // blocks
    chunks = units // CHUNK
    part = units // groups
    all_rows = groups * rows

    def share_of(member, column):
        return (member - pick(column, turns) + groups) % groups

    def member_of(share, column):
        return (share + pick(column, turns)) % groups

    mine = share_of(dp, me)
    my_offset = pick(mine, order)
    partner = (me + my_offset) % n
    askers = [(me - order[k] + n) % n for k in range(groups)]
    ask_member = [member_of(k, askers[k]) for k in range(groups)]
    others = [(dp + r) % groups for r in range(1, groups)]

    barrier = pltpu.get_barrier_semaphore()
    greeted = [(other, me) for other in others]
    greeted += [(ask_member[k], askers[k]) for k in range(groups)]
    greeted += [(member, partner) for member in range(groups)]
    for device in greeted:
        pl.semaphore_signal(barrier, inc=1, device_id=device, device_id_type=MESH)

    load = pltpu.make_async_copy(codes_ref, codes, load_sem)
    load.start()

    def slot_of(offset):
        slot = 0
        for s in range(groups):
            slot = slot + jnp.where(pairs_ref[1, s] // per_device == offset, s, 0)
        return slot

    def chosen(column, slot, side):
        return lax.rem(pairs_ref[side, groups * column + slot], per_device)

    my_rows = pl.ds(pl.multiple_of(dp * rows, rows), rows)
    right_pick = [chosen(askers[k], slot_of(order[k]), 1) for k in range(groups)]
    left_pick = [
        chosen(me, slot_of(pick(share_of(member, me), order)), 0) for member in others + [dp]
    ]
    factors = [scales_ref[:, expert, :].T for expert in range(per_device)]

    def scale_and_stage(c):
        for expert in range(per_device):
            for block in range(c * CHUNK // width, (c + 1) * CHUNK // width):
                at = slice(block * width, (block + 1) * width)
                inside = slice(block * width - c * CHUNK, (block + 1) * width - c * CHUNK)
                acts[expert, c, :, inside] = (
                    codes[expert, :, at].astype(jnp.float32) * factors[expert][:, block : block + 1]
                ).astype(jnp.bfloat16)
        for k in range(groups):
            send_right[k, c] = acts[right_pick[k], c]
        for r in range(groups - 1):
            send_left[r, c] = acts[left_pick[r], c]
        left_rows[c, my_rows, :] = acts[left_pick[-1], c]

    def left_copy(r, c):
        return pltpu.make_async_remote_copy(
            src_ref=send_left.at[r, c],
            dst_ref=left_rows.at[c, my_rows, :],
            send_sem=left_send_sem.at[r, c],
            recv_sem=left_sem.at[c, dp],
            device_id=(others[r], me),
            device_id_type=MESH,
        )

    def right_copy(k, c):
        return pltpu.make_async_remote_copy(
            src_ref=send_right.at[k, c],
            dst_ref=right_rows.at[c, my_rows, :],
            send_sem=right_send_sem.at[k, c],
            recv_sem=right_sem.at[c, dp],
            device_id=(ask_member[k], askers[k]),
            device_id_type=MESH,
        )

    load.wait()
    ahead = (2 * chunks + 2) // 3
    staged = 0
    for c in range(chunks):
        lefts = range(c * chunks // ahead, (c + 1) * chunks // ahead) if c < ahead else range(0)
        while staged <= max([c, *lefts]):
            scale_and_stage(staged)
            staged += 1
        if c == 0:
            pl.semaphore_wait(barrier, len(greeted))
        for k in range(groups):
            right_copy(k, c).start()
        for at in lefts:
            for r in range(groups - 1):
                left_copy(r, at).start()

    best[...] = jnp.full_like(best, -jnp.inf)
    for i in range(chunks):
        at = slice(i * CHUNK, (i + 1) * CHUNK)
        for other in others:
            theirs = pl.ds(pl.multiple_of(other * rows, rows), rows)
            pltpu.make_async_remote_copy(
                src_ref=send_left.at[0, 0],
                dst_ref=left_rows.at[i, theirs, :],
                send_sem=left_send_sem.at[0, 0],
                recv_sem=left_sem.at[i, other],
                device_id=(other, me),
                device_id_type=MESH,
            ).wait_recv()
        block = left_rows[i]
        wide = block.astype(jnp.float32)
        square = jnp.sum(wide * wide, axis=0, keepdims=True) / all_rows
        inverse = 1.0 / jnp.sqrt(square + EPSILON)
        inv_left[at, :] = jnp.broadcast_to(inverse, (128, CHUNK)).T
        turned[at, :] = block.T

    @pl.loop(0, chunks)
    def _(c):
        for member in range(groups):
            pltpu.make_async_remote_copy(
                src_ref=send_right.at[0, 0],
                dst_ref=right_rows.at[c, pl.ds(member * rows, rows), :],
                send_sem=right_send_sem.at[0, 0],
                recv_sem=right_sem.at[c, member],
                device_id=(member, partner),
                device_id_type=MESH,
            ).wait_recv()
        block = right_rows[c]
        wide = block.astype(jnp.float32)
        square = jnp.sum(wide * wide, axis=0, keepdims=True) / all_rows
        inverse = 1.0 / jnp.sqrt(square + EPSILON)
        tops = [jnp.full((8, 128), -jnp.inf, jnp.float32) for _ in range(CHUNK // 128)]
        for i in range(chunks):
            at = slice(i * CHUNK, (i + 1) * CHUNK)
            gram = jnp.dot(turned[at, :], block, preferred_element_type=jnp.float32)
            scale = inv_left[at, :]
            running = best[at, :]
            for h in range(CHUNK // 128):
                lanes = slice(h * 128, (h + 1) * 128)
                scaled = gram[:, lanes] * scale
                running = jnp.maximum(running, scaled * inverse[:, lanes])
                gram_top = jnp.max(scaled.reshape(CHUNK // 8, 8, 128), axis=0)
                tops[h] = jnp.maximum(tops[h], gram_top)
            best[at, :] = running
        top = jnp.max(jnp.concatenate(tops, axis=1), axis=0, keepdims=True)
        right_row[c] = top * inverse / all_rows

    right_full = jnp.concatenate([right_row[c] for c in range(chunks)], axis=1)
    left_full = jnp.concatenate(
        [
            jnp.max(best[i * CHUNK : (i + 1) * CHUNK, :].T, axis=0, keepdims=True)
            for i in range(chunks)
        ],
        axis=1,
    ) / all_rows
    for member in range(groups):
        at = slice(member * part, (member + 1) * part)
        right_stage[member] = right_full[:, at]
        left_stage[member] = left_full[:, at]

    def right_result(member):
        return pltpu.make_async_remote_copy(
            src_ref=right_stage.at[member],
            dst_ref=right_got.at[mine],
            send_sem=out_send_sem.at[member],
            recv_sem=right_got_sem.at[mine],
            device_id=(member, partner),
            device_id_type=MESH,
        )

    def left_result(r):
        return pltpu.make_async_remote_copy(
            src_ref=left_stage.at[others[r]],
            dst_ref=left_got.at[mine],
            send_sem=out_send_sem.at[groups + r],
            recv_sem=left_got_sem.at[mine],
            device_id=(others[r], me),
            device_id_type=MESH,
        )

    for member in range(groups):
        right_result(member).start()
    for r in range(groups - 1):
        left_result(r).start()
    left_got[mine] = left_stage[dp]

    @pl.loop(0, chunks)
    def _(c):
        for r in range(groups - 1):
            left_copy(r, c).wait_send()
        for k in range(groups):
            right_copy(k, c).wait_send()

    for other in others:
        share = share_of(other, me)
        pltpu.make_async_remote_copy(
            src_ref=left_stage.at[0],
            dst_ref=left_got.at[share],
            send_sem=out_send_sem.at[0],
            recv_sem=left_got_sem.at[share],
            device_id=(other, me),
            device_id_type=MESH,
        ).wait_recv()
    for k in range(groups):
        pltpu.make_async_remote_copy(
            src_ref=right_stage.at[0],
            dst_ref=right_got.at[k],
            send_sem=out_send_sem.at[0],
            recv_sem=right_got_sem.at[k],
            device_id=(ask_member[k], askers[k]),
            device_id_type=MESH,
        ).wait_recv()
    for member in range(groups):
        right_result(member).wait_send()
    for r in range(groups - 1):
        left_result(r).wait_send()

    for s in range(groups):
        offset = pairs_ref[1, s] // per_device
        share = 0
        for k in range(groups):
            share = share + jnp.where(offset == order[k], k, 0)
        out_ref[s : s + 1, :] = left_got[share]
        out_ref[groups + s : groups + s + 1, :] = right_got[share]


def pair_call(order, turns, n, groups, collective_id, unit_codes, block_scales, pairs):
    per_device, rows, units = unit_codes.shape
    chunks = units // CHUNK
    part = units // groups
    out = jax.ShapeDtypeStruct((2 * groups, part), jnp.float32)
    vmem = pl.BlockSpec(memory_space=pltpu.VMEM)
    dma = pltpu.SemaphoreType.DMA
    return pl.pallas_call(
        functools.partial(pair_kernel, order, turns, n, groups),
        out_shape=out,
        in_specs=[pl.BlockSpec(memory_space=pl.ANY), vmem, pl.BlockSpec(memory_space=pltpu.SMEM)],
        out_specs=vmem,
        scratch_shapes=[
            pltpu.VMEM((per_device, rows, units), jnp.bfloat16),
            pltpu.VMEM((per_device, chunks, rows, CHUNK), jnp.bfloat16),
            pltpu.VMEM((groups - 1, chunks, rows, CHUNK), jnp.bfloat16),
            pltpu.VMEM((groups, chunks, rows, CHUNK), jnp.bfloat16),
            pltpu.VMEM((chunks, groups * rows, CHUNK), jnp.bfloat16),
            pltpu.VMEM((chunks, groups * rows, CHUNK), jnp.bfloat16),
            pltpu.VMEM((units, groups * rows), jnp.bfloat16),
            pltpu.VMEM((units, 128), jnp.float32),
            pltpu.VMEM((units, 128), jnp.float32),
            pltpu.VMEM((chunks, 1, CHUNK), jnp.float32),
            pltpu.VMEM((groups, 1, part), jnp.float32),
            pltpu.VMEM((groups, 1, part), jnp.float32),
            pltpu.VMEM((groups, 1, part), jnp.float32),
            pltpu.VMEM((groups, 1, part), jnp.float32),
            dma,
            dma((groups - 1, chunks)),
            dma((chunks, groups)),
            dma((groups, chunks)),
            dma((chunks, groups)),
            dma((2 * groups - 1,)),
            dma((groups,)),
            dma((groups,)),
        ],
        compiler_params=pltpu.CompilerParams(
            collective_id=collective_id, has_side_effects=True, vmem_limit_bytes=56 * 2**20
        ),
        cost_estimate=pl.CostEstimate(
            flops=2 * units * units * groups * rows, bytes_accessed=2 * units * rows * per_device, transcendentals=0
        ),
    )(unit_codes, jnp.transpose(block_scales, (1, 0, 2)), pairs)


def offset_sets(n, slots):
    fixed = sorted({1, n // 2, n - 1})
    rest = [o for o in range(1, n) if o not in fixed]
    free = slots - len(fixed)
    if free < 0 or math.comb(len(rest), free) > MAX_BRANCHES:
        return []
    return [tuple(sorted(fixed + list(more))) for more in itertools.combinations(rest, free)]


def body(unit_codes, block_scales, pair_list):
    n = lax.axis_size("expert")
    groups = lax.axis_size("dp")
    per_device, rows, units = unit_codes.shape
    slots = pair_list.shape[0] // n
    sets = offset_sets(n, slots)
    fits = (
        slots == groups
        and rows % 16 == 0
        and units % CHUNK == 0
        and CHUNK % (units // block_scales.shape[1]) == 0
        and units // block_scales.shape[1] % 128 == 0
        and units % (128 * groups) == 0
        and (groups * rows) % 128 == 0
    )
    if not sets or not fits:
        return general_body(unit_codes, block_scales, pair_list)
    columns = pair_list.T
    offsets = pair_list[:slots, 1] // per_device
    if slots == 4 and n > 4:
        free = [(sum(members) - 1 - n // 2 - (n - 1), at) for at, members in enumerate(sets)]
        side = lax.broadcasted_iota(jnp.int32, columns.shape, 0)
        slot = lax.broadcasted_iota(jnp.int32, columns.shape, 1)
        offsets = jnp.where((side == 1) & (slot < slots), columns // per_device, 0)
        branch = jnp.sum(sum(jnp.where(offsets == offset, at, 0) for offset, at in free))
        columns = jnp.where(side == 0, columns % per_device, columns)
        branch, columns = lax.optimization_barrier((branch, columns))
    else:
        branch = 0
        for at, members in enumerate(sets):
            same = jnp.all(jnp.any(offsets[:, None] == jnp.asarray(members)[None, :], axis=1))
            branch = branch + jnp.where(same, at, 0)
    calls = []
    for at, members in enumerate(sets):
        order, turns = TURNS.get(members, (members, (0,) * n)) if (n, groups) == (8, 4) else (members, (0,) * n)
        calls.append(functools.partial(pair_call, order, turns, n, groups, at))
    best = lax.switch(branch, calls, unit_codes, block_scales, columns)
    return (best[None, :slots], best[None, slots:])


def solution(mesh):
    in_specs = (P("expert", "dp", None), P("expert", None, "dp"), P())
    out_specs = (P("expert", None, "dp"), P("expert", None, "dp"))
    return jax.shard_map(body, mesh=mesh, in_specs=in_specs, out_specs=out_specs, check_vma=False)
```

```python
import functools
import itertools
import math

import jax
import jax.numpy as jnp
from jax import lax
from jax.experimental import pallas as pl
from jax.experimental.pallas import tpu as pltpu
from jax.sharding import PartitionSpec as P

EPSILON = 1e-06


def general_body(unit_codes, block_scales, pair_list):
    num_devices = lax.axis_size("expert")
    groups = lax.axis_size("dp")
    my_index = lax.axis_index("expert")
    dp_index = lax.axis_index("dp")
    per_device, row_count, unit_count = unit_codes.shape
    num_blocks = block_scales.shape[1]
    block_len = unit_count // num_blocks
    slice_width = unit_count // groups
    factor = jnp.transpose(block_scales, (0, 2, 1))[:, :, :, None]
    acts = (
        unit_codes.astype(jnp.float32).reshape(per_device, row_count, num_blocks, block_len)
        * factor
    )
    acts = acts.reshape(per_device, row_count, unit_count).astype(jnp.bfloat16)
    slot_count = pair_list.shape[0] // num_devices
    pair_table = pair_list.reshape(num_devices, slot_count, 2)
    my_pairs = lax.dynamic_index_in_dim(pair_table, my_index, 0, keepdims=False)
    left_local = my_pairs[:, 0] % per_device
    right_dev = my_pairs[:, 1] // per_device
    is_asked = pair_table[:, :, 1] // per_device == my_index
    chosen = jnp.sum(jnp.where(is_asked, pair_table[:, :, 1] % per_device, 0), axis=1)
    in_use = jnp.any(is_asked, axis=1)
    chooser = ((chosen[:, None] == jnp.arange(per_device)[None, :]) & in_use[:, None]).astype(
        jnp.bfloat16
    )
    own_full = lax.all_gather(acts, "dp", axis=1, tiled=True)
    flattened = acts.reshape(per_device, -1)
    outbound = jnp.dot(chooser, flattened, preferred_element_type=jnp.float32).astype(jnp.bfloat16)
    received = lax.all_to_all(
        outbound.reshape((num_devices,) + acts.shape[1:]),
        "expert",
        split_axis=0,
        concat_axis=0,
        tiled=True,
    )
    wanted = jnp.take(received, right_dev, axis=0)
    partner = lax.all_to_all(wanted, "dp", split_axis=2, concat_axis=1, tiled=True)
    all_rows = partner.shape[1]
    own_square = (
        jnp.einsum("era,era->ea", own_full, own_full, preferred_element_type=jnp.float32) / all_rows
    )
    inv_own = 1.0 / jnp.sqrt(own_square + EPSILON)
    part_square = (
        jnp.einsum("srb,srb->sb", partner, partner, preferred_element_type=jnp.float32) / all_rows
    )
    inv_part = 1.0 / jnp.sqrt(part_square + EPSILON)

    def single(member):
        expert_pick, partner_block, inv_unit = member
        left_rows = jnp.take(own_full, expert_pick, axis=0)
        gram_block = jnp.einsum(
            "ra,rb->ab", left_rows, partner_block, preferred_element_type=jnp.float32
        )
        correlation = (
            gram_block
            / all_rows
            * jnp.take(inv_own, expert_pick, axis=0)[:, None]
            * inv_unit[None, :]
        )
        return (jnp.max(correlation, axis=1), jnp.max(correlation, axis=0))

    def several(member):
        return jax.vmap(single)(member)

    bundle = math.gcd(slot_count, 4)
    stacked = (
        left_local.reshape(-1, bundle),
        partner.reshape(-1, bundle, all_rows, slice_width),
        inv_part.reshape(-1, bundle, slice_width),
    )
    left_part, right_part = lax.map(several, stacked)
    left_part = left_part.reshape(slot_count, unit_count)
    right_part = right_part.reshape(slot_count, slice_width)
    left_all = lax.pmax(left_part, "dp")
    left_out = lax.dynamic_slice_in_dim(left_all, dp_index * slice_width, slice_width, 1)
    target = (right_dev[:, None] == jnp.arange(num_devices)[None, :]).astype(jnp.float32)
    outgoing = jnp.dot(
        target.T, right_part, precision=lax.Precision.HIGHEST, preferred_element_type=jnp.float32
    )
    returned = lax.all_to_all(outgoing, "expert", split_axis=0, concat_axis=0, tiled=True)
    offsets = pair_table[0, :, 1] // per_device
    source_dev = (my_index - offsets) % num_devices
    right_out = jnp.take(returned, source_dev, axis=0)
    return (left_out[None], right_out[None])


MESH = pl.DeviceIdType.MESH
CHUNK = 256
MAX_BRANCHES = 8
TURNS = {
    (1, 2, 4, 7): ((1, 7, 4, 2), (1, 1, 2, 2, 0, 3, 1, 0)),
    (1, 3, 4, 7): ((1, 4, 7, 3), (0, 1, 3, 0, 3, 1, 2, 0)),
    (1, 4, 5, 7): ((1, 4, 7, 5), (0, 0, 1, 3, 3, 2, 1, 2)),
    (1, 4, 6, 7): ((1, 7, 6, 4), (0, 2, 1, 3, 2, 3, 3, 0)),
}


def pick(index, table):
    total = 0
    size = len(table)
    for at, value in enumerate(table):
        if value:
            apart = (index - at) * (index - at)
            total = total + value * (1 - (apart + size * size - 1) // (size * size))
    return total


def pair_kernel(
    order, turns, n, groups,
    codes_ref, scales_hbm, pairs_hbm, out_ref,
    scales_ref, pairs_ref, codes, acts, send_left, send_right, left_rows, right_rows, turned, inv_left, best, right_row,
    left_stage, right_stage, left_got, right_got,
    load_sem, scales_sem, pairs_sem, left_send_sem, left_sem, right_send_sem, right_sem, out_send_sem, left_got_sem, right_got_sem,
):
    me = lax.axis_index("expert")
    dp = lax.axis_index("dp")
    per_device, rows, units = codes_ref.shape
    blocks = scales_hbm.shape[0]
    width = units // blocks
    chunks = units // CHUNK
    part = units // groups
    all_rows = groups * rows

    def share_of(member, column):
        return (member - pick(column, turns) + groups) % groups

    def member_of(share, column):
        return (share + pick(column, turns)) % groups

    mine = share_of(dp, me)
    my_offset = pick(mine, order)
    partner = (me + my_offset) % n
    askers = [(me - order[k] + n) % n for k in range(groups)]
    ask_member = [member_of(k, askers[k]) for k in range(groups)]
    others = [(dp + r) % groups for r in range(1, groups)]

    barrier = pltpu.get_barrier_semaphore()
    greeted = [(other, me) for other in others]
    greeted += [(ask_member[k], askers[k]) for k in range(groups)]
    greeted += [(member, partner) for member in range(groups)]
    for device in greeted:
        pl.semaphore_signal(barrier, inc=1, device_id=device, device_id_type=MESH)

    load = pltpu.make_async_copy(codes_ref, codes, load_sem)
    load_scales = pltpu.make_async_copy(scales_hbm, scales_ref, scales_sem)
    load_pairs = pltpu.make_async_copy(pairs_hbm, pairs_ref, pairs_sem)
    load_pairs.start()
    load_scales.start()
    load.start()
    load_pairs.wait()

    def slot_of(offset):
        slot = 0
        for s in range(groups):
            slot = slot + jnp.where(pairs_ref[1, s] // per_device == offset, s, 0)
        return slot

    def chosen(column, slot, side):
        return lax.rem(pairs_ref[side, groups * column + slot], per_device)

    my_rows = pl.ds(pl.multiple_of(dp * rows, rows), rows)
    right_pick = [chosen(askers[k], slot_of(order[k]), 1) for k in range(groups)]
    left_pick = [
        chosen(me, slot_of(pick(share_of(member, me), order)), 0) for member in others + [dp]
    ]
    load_scales.wait()
    factors = [scales_ref[:, expert, :].T for expert in range(per_device)]

    def scale_and_stage(c):
        for expert in range(per_device):
            for block in range(c * CHUNK // width, (c + 1) * CHUNK // width):
                at = slice(block * width, (block + 1) * width)
                inside = slice(block * width - c * CHUNK, (block + 1) * width - c * CHUNK)
                acts[expert, c, :, inside] = (
                    codes[expert, :, at].astype(jnp.float32) * factors[expert][:, block : block + 1]
                ).astype(jnp.bfloat16)
        for k in range(groups):
            send_right[k, c] = acts[right_pick[k], c]
        for r in range(groups - 1):
            send_left[r, c] = acts[left_pick[r], c]
        left_rows[c, my_rows, :] = acts[left_pick[-1], c]

    def left_copy(r, c):
        return pltpu.make_async_remote_copy(
            src_ref=send_left.at[r, c],
            dst_ref=left_rows.at[c, my_rows, :],
            send_sem=left_send_sem.at[r, c],
            recv_sem=left_sem.at[c, dp],
            device_id=(others[r], me),
            device_id_type=MESH,
        )

    def right_copy(k, c):
        return pltpu.make_async_remote_copy(
            src_ref=send_right.at[k, c],
            dst_ref=right_rows.at[c, my_rows, :],
            send_sem=right_send_sem.at[k, c],
            recv_sem=right_sem.at[c, dp],
            device_id=(ask_member[k], askers[k]),
            device_id_type=MESH,
        )

    load.wait()
    ahead = (2 * chunks + 2) // 3
    staged = 0
    for c in range(chunks):
        lefts = range(c * chunks // ahead, (c + 1) * chunks // ahead) if c < ahead else range(0)
        while staged <= max([c, *lefts]):
            scale_and_stage(staged)
            staged += 1
        if c == 0:
            pl.semaphore_wait(barrier, len(greeted))
        for k in range(groups):
            right_copy(k, c).start()
        for at in lefts:
            for r in range(groups - 1):
                left_copy(r, at).start()

    best[...] = jnp.full_like(best, -jnp.inf)
    for i in range(chunks):
        at = slice(i * CHUNK, (i + 1) * CHUNK)
        for other in others:
            theirs = pl.ds(pl.multiple_of(other * rows, rows), rows)
            pltpu.make_async_remote_copy(
                src_ref=send_left.at[0, 0],
                dst_ref=left_rows.at[i, theirs, :],
                send_sem=left_send_sem.at[0, 0],
                recv_sem=left_sem.at[i, other],
                device_id=(other, me),
                device_id_type=MESH,
            ).wait_recv()
        block = left_rows[i]
        wide = block.astype(jnp.float32)
        square = jnp.sum(wide * wide, axis=0, keepdims=True) / all_rows
        inverse = 1.0 / jnp.sqrt(square + EPSILON)
        inv_left[at, :] = jnp.broadcast_to(inverse, (128, CHUNK)).T
        turned[at, :] = block.T

    @pl.loop(0, chunks)
    def _(c):
        for member in range(groups):
            pltpu.make_async_remote_copy(
                src_ref=send_right.at[0, 0],
                dst_ref=right_rows.at[c, pl.ds(member * rows, rows), :],
                send_sem=right_send_sem.at[0, 0],
                recv_sem=right_sem.at[c, member],
                device_id=(member, partner),
                device_id_type=MESH,
            ).wait_recv()
        block = right_rows[c]
        wide = block.astype(jnp.float32)
        square = jnp.sum(wide * wide, axis=0, keepdims=True) / all_rows
        inverse = 1.0 / jnp.sqrt(square + EPSILON)
        tops = [jnp.full((8, 128), -jnp.inf, jnp.float32) for _ in range(CHUNK // 128)]
        for i in range(chunks):
            at = slice(i * CHUNK, (i + 1) * CHUNK)
            gram = jnp.dot(turned[at, :], block, preferred_element_type=jnp.float32)
            scale = inv_left[at, :]
            running = best[at, :]
            for h in range(CHUNK // 128):
                lanes = slice(h * 128, (h + 1) * 128)
                scaled = gram[:, lanes] * scale
                running = jnp.maximum(running, scaled * inverse[:, lanes])
                gram_top = jnp.max(scaled.reshape(CHUNK // 8, 8, 128), axis=0)
                tops[h] = jnp.maximum(tops[h], gram_top)
            best[at, :] = running
        top = jnp.max(jnp.concatenate(tops, axis=1), axis=0, keepdims=True)
        right_row[c] = top * inverse / all_rows

    right_full = jnp.concatenate([right_row[c] for c in range(chunks)], axis=1)
    left_full = jnp.concatenate(
        [
            jnp.max(best[i * CHUNK : (i + 1) * CHUNK, :].T, axis=0, keepdims=True)
            for i in range(chunks)
        ],
        axis=1,
    ) / all_rows
    for member in range(groups):
        at = slice(member * part, (member + 1) * part)
        right_stage[member] = right_full[:, at]
        left_stage[member] = left_full[:, at]

    def right_result(member):
        return pltpu.make_async_remote_copy(
            src_ref=right_stage.at[member],
            dst_ref=right_got.at[mine],
            send_sem=out_send_sem.at[member],
            recv_sem=right_got_sem.at[mine],
            device_id=(member, partner),
            device_id_type=MESH,
        )

    def left_result(r):
        return pltpu.make_async_remote_copy(
            src_ref=left_stage.at[others[r]],
            dst_ref=left_got.at[mine],
            send_sem=out_send_sem.at[groups + r],
            recv_sem=left_got_sem.at[mine],
            device_id=(others[r], me),
            device_id_type=MESH,
        )

    for member in range(groups):
        right_result(member).start()
    for r in range(groups - 1):
        left_result(r).start()
    left_got[mine] = left_stage[dp]

    @pl.loop(0, chunks)
    def _(c):
        for r in range(groups - 1):
            left_copy(r, c).wait_send()
        for k in range(groups):
            right_copy(k, c).wait_send()

    for other in others:
        share = share_of(other, me)
        pltpu.make_async_remote_copy(
            src_ref=left_stage.at[0],
            dst_ref=left_got.at[share],
            send_sem=out_send_sem.at[0],
            recv_sem=left_got_sem.at[share],
            device_id=(other, me),
            device_id_type=MESH,
        ).wait_recv()
    for k in range(groups):
        pltpu.make_async_remote_copy(
            src_ref=right_stage.at[0],
            dst_ref=right_got.at[k],
            send_sem=out_send_sem.at[0],
            recv_sem=right_got_sem.at[k],
            device_id=(ask_member[k], askers[k]),
            device_id_type=MESH,
        ).wait_recv()
    for member in range(groups):
        right_result(member).wait_send()
    for r in range(groups - 1):
        left_result(r).wait_send()

    for s in range(groups):
        offset = pairs_ref[1, s] // per_device
        share = 0
        for k in range(groups):
            share = share + jnp.where(offset == order[k], k, 0)
        out_ref[s : s + 1, :] = left_got[share]
        out_ref[groups + s : groups + s + 1, :] = right_got[share]


def pair_call(order, turns, n, groups, collective_id, unit_codes, block_scales, pairs):
    per_device, rows, units = unit_codes.shape
    chunks = units // CHUNK
    part = units // groups
    out = jax.ShapeDtypeStruct((2 * groups, part), jnp.float32)
    anywhere = pl.BlockSpec(memory_space=pl.ANY)
    dma = pltpu.SemaphoreType.DMA
    return pl.pallas_call(
        functools.partial(pair_kernel, order, turns, n, groups),
        out_shape=out,
        in_specs=[anywhere, anywhere, anywhere],
        out_specs=pl.BlockSpec(memory_space=pltpu.VMEM),
        scratch_shapes=[
            pltpu.VMEM((block_scales.shape[1], per_device, rows), jnp.float32),
            pltpu.SMEM(pairs.shape, jnp.int32),
            pltpu.VMEM((per_device, rows, units), jnp.bfloat16),
            pltpu.VMEM((per_device, chunks, rows, CHUNK), jnp.bfloat16),
            pltpu.VMEM((groups - 1, chunks, rows, CHUNK), jnp.bfloat16),
            pltpu.VMEM((groups, chunks, rows, CHUNK), jnp.bfloat16),
            pltpu.VMEM((chunks, groups * rows, CHUNK), jnp.bfloat16),
            pltpu.VMEM((chunks, groups * rows, CHUNK), jnp.bfloat16),
            pltpu.VMEM((units, groups * rows), jnp.bfloat16),
            pltpu.VMEM((units, 128), jnp.float32),
            pltpu.VMEM((units, 128), jnp.float32),
            pltpu.VMEM((chunks, 1, CHUNK), jnp.float32),
            pltpu.VMEM((groups, 1, part), jnp.float32),
            pltpu.VMEM((groups, 1, part), jnp.float32),
            pltpu.VMEM((groups, 1, part), jnp.float32),
            pltpu.VMEM((groups, 1, part), jnp.float32),
            dma,
            dma,
            dma,
            dma((groups - 1, chunks)),
            dma((chunks, groups)),
            dma((groups, chunks)),
            dma((chunks, groups)),
            dma((2 * groups - 1,)),
            dma((groups,)),
            dma((groups,)),
        ],
        compiler_params=pltpu.CompilerParams(
            collective_id=collective_id, has_side_effects=True, vmem_limit_bytes=56 * 2**20
        ),
        cost_estimate=pl.CostEstimate(
            flops=2 * units * units * groups * rows, bytes_accessed=2 * units * rows * per_device, transcendentals=0
        ),
    )(unit_codes, jnp.transpose(block_scales, (1, 0, 2)), pairs)


def offset_sets(n, slots):
    fixed = sorted({1, n // 2, n - 1})
    rest = [o for o in range(1, n) if o not in fixed]
    free = slots - len(fixed)
    if free < 0 or math.comb(len(rest), free) > MAX_BRANCHES:
        return []
    return [tuple(sorted(fixed + list(more))) for more in itertools.combinations(rest, free)]


def body(unit_codes, block_scales, pair_list):
    n = lax.axis_size("expert")
    groups = lax.axis_size("dp")
    per_device, rows, units = unit_codes.shape
    slots = pair_list.shape[0] // n
    sets = offset_sets(n, slots)
    fits = (
        slots == groups
        and rows % 16 == 0
        and units % CHUNK == 0
        and CHUNK % (units // block_scales.shape[1]) == 0
        and units // block_scales.shape[1] % 128 == 0
        and units % (128 * groups) == 0
        and (groups * rows) % 128 == 0
    )
    if not sets or not fits:
        return general_body(unit_codes, block_scales, pair_list)
    columns = pair_list.T
    offsets = pair_list[:slots, 1] // per_device
    if slots == 4 and n > 4:
        free = [(sum(members) - 1 - n // 2 - (n - 1), at) for at, members in enumerate(sets)]
        side = lax.broadcasted_iota(jnp.int32, columns.shape, 0)
        slot = lax.broadcasted_iota(jnp.int32, columns.shape, 1)
        offsets = jnp.where((side == 1) & (slot < slots), columns // per_device, 0)
        branch = jnp.sum(sum(jnp.where(offsets == offset, at, 0) for offset, at in free))
        columns = jnp.where(side == 0, columns % per_device, columns)
        branch, columns = lax.optimization_barrier((branch, columns))
    else:
        branch = 0
        for at, members in enumerate(sets):
            same = jnp.all(jnp.any(offsets[:, None] == jnp.asarray(members)[None, :], axis=1))
            branch = branch + jnp.where(same, at, 0)
    calls = []
    for at, members in enumerate(sets):
        order, turns = TURNS.get(members, (members, (0,) * n)) if (n, groups) == (8, 4) else (members, (0,) * n)
        calls.append(functools.partial(pair_call, order, turns, n, groups, at))
    best = lax.switch(branch, calls, unit_codes, block_scales, columns)
    return (best[None, :slots], best[None, slots:])


def solution(mesh):
    in_specs = (P("expert", "dp", None), P("expert", None, "dp"), P())
    out_specs = (P("expert", None, "dp"), P("expert", None, "dp"))
    return jax.shard_map(body, mesh=mesh, in_specs=in_specs, out_specs=out_specs, check_vma=False)
```

```python
import functools
import itertools
import math

import jax
import jax.numpy as jnp
from jax import lax
from jax.experimental import pallas as pl
from jax.experimental.pallas import tpu as pltpu
from jax.sharding import PartitionSpec as P

EPSILON = 1e-06


def general_body(unit_codes, block_scales, pair_list):
    num_devices = lax.axis_size("expert")
    groups = lax.axis_size("dp")
    my_index = lax.axis_index("expert")
    dp_index = lax.axis_index("dp")
    per_device, row_count, unit_count = unit_codes.shape
    num_blocks = block_scales.shape[1]
    block_len = unit_count // num_blocks
    slice_width = unit_count // groups
    factor = jnp.transpose(block_scales, (0, 2, 1))[:, :, :, None]
    acts = (
        unit_codes.astype(jnp.float32).reshape(per_device, row_count, num_blocks, block_len)
        * factor
    )
    acts = acts.reshape(per_device, row_count, unit_count).astype(jnp.bfloat16)
    slot_count = pair_list.shape[0] // num_devices
    pair_table = pair_list.reshape(num_devices, slot_count, 2)
    my_pairs = lax.dynamic_index_in_dim(pair_table, my_index, 0, keepdims=False)
    left_local = my_pairs[:, 0] % per_device
    right_dev = my_pairs[:, 1] // per_device
    is_asked = pair_table[:, :, 1] // per_device == my_index
    chosen = jnp.sum(jnp.where(is_asked, pair_table[:, :, 1] % per_device, 0), axis=1)
    in_use = jnp.any(is_asked, axis=1)
    chooser = ((chosen[:, None] == jnp.arange(per_device)[None, :]) & in_use[:, None]).astype(
        jnp.bfloat16
    )
    own_full = lax.all_gather(acts, "dp", axis=1, tiled=True)
    flattened = acts.reshape(per_device, -1)
    outbound = jnp.dot(chooser, flattened, preferred_element_type=jnp.float32).astype(jnp.bfloat16)
    received = lax.all_to_all(
        outbound.reshape((num_devices,) + acts.shape[1:]),
        "expert",
        split_axis=0,
        concat_axis=0,
        tiled=True,
    )
    wanted = jnp.take(received, right_dev, axis=0)
    partner = lax.all_to_all(wanted, "dp", split_axis=2, concat_axis=1, tiled=True)
    all_rows = partner.shape[1]
    own_square = (
        jnp.einsum("era,era->ea", own_full, own_full, preferred_element_type=jnp.float32) / all_rows
    )
    inv_own = 1.0 / jnp.sqrt(own_square + EPSILON)
    part_square = (
        jnp.einsum("srb,srb->sb", partner, partner, preferred_element_type=jnp.float32) / all_rows
    )
    inv_part = 1.0 / jnp.sqrt(part_square + EPSILON)

    def single(member):
        expert_pick, partner_block, inv_unit = member
        left_rows = jnp.take(own_full, expert_pick, axis=0)
        gram_block = jnp.einsum(
            "ra,rb->ab", left_rows, partner_block, preferred_element_type=jnp.float32
        )
        correlation = (
            gram_block
            / all_rows
            * jnp.take(inv_own, expert_pick, axis=0)[:, None]
            * inv_unit[None, :]
        )
        return (jnp.max(correlation, axis=1), jnp.max(correlation, axis=0))

    def several(member):
        return jax.vmap(single)(member)

    bundle = math.gcd(slot_count, 4)
    stacked = (
        left_local.reshape(-1, bundle),
        partner.reshape(-1, bundle, all_rows, slice_width),
        inv_part.reshape(-1, bundle, slice_width),
    )
    left_part, right_part = lax.map(several, stacked)
    left_part = left_part.reshape(slot_count, unit_count)
    right_part = right_part.reshape(slot_count, slice_width)
    left_all = lax.pmax(left_part, "dp")
    left_out = lax.dynamic_slice_in_dim(left_all, dp_index * slice_width, slice_width, 1)
    target = (right_dev[:, None] == jnp.arange(num_devices)[None, :]).astype(jnp.float32)
    outgoing = jnp.dot(
        target.T, right_part, precision=lax.Precision.HIGHEST, preferred_element_type=jnp.float32
    )
    returned = lax.all_to_all(outgoing, "expert", split_axis=0, concat_axis=0, tiled=True)
    offsets = pair_table[0, :, 1] // per_device
    source_dev = (my_index - offsets) % num_devices
    right_out = jnp.take(returned, source_dev, axis=0)
    return (left_out[None], right_out[None])


MESH = pl.DeviceIdType.MESH
CHUNK = 256
MAX_BRANCHES = 8
TURNS = {
    (1, 2, 4, 7): ((1, 7, 4, 2), (1, 1, 2, 2, 0, 3, 1, 0)),
    (1, 3, 4, 7): ((1, 4, 7, 3), (0, 1, 3, 0, 3, 1, 2, 0)),
    (1, 4, 5, 7): ((1, 4, 7, 5), (0, 0, 1, 3, 3, 2, 1, 2)),
    (1, 4, 6, 7): ((1, 7, 6, 4), (0, 2, 1, 3, 2, 3, 3, 0)),
}


def pick(index, table):
    total = 0
    size = len(table)
    for at, value in enumerate(table):
        if value:
            apart = (index - at) * (index - at)
            total = total + value * (1 - (apart + size * size - 1) // (size * size))
    return total


def pair_kernel(
    order, turns, n, groups,
    codes_ref, scales_hbm, pairs_hbm, out_ref,
    scales_ref, pairs_ref, codes, acts, send_left, send_right, left_rows, right_rows, turned, inv_left, best, right_row,
    left_stage, right_stage, left_got, right_got,
    load_sem, scales_sem, pairs_sem, left_send_sem, left_sem, right_send_sem, right_sem, out_send_sem, left_got_sem, right_got_sem,
):
    me = lax.axis_index("expert")
    dp = lax.axis_index("dp")
    per_device, rows, units = codes_ref.shape
    blocks = scales_hbm.shape[0]
    width = units // blocks
    chunks = units // CHUNK
    part = units // groups
    all_rows = groups * rows

    def share_of(member, column):
        return (member - pick(column, turns) + groups) % groups

    def member_of(share, column):
        return (share + pick(column, turns)) % groups

    mine = share_of(dp, me)
    my_offset = pick(mine, order)
    partner = (me + my_offset) % n
    askers = [(me - order[k] + n) % n for k in range(groups)]
    ask_member = [member_of(k, askers[k]) for k in range(groups)]
    others = [(dp + r) % groups for r in range(1, groups)]

    barrier = pltpu.get_barrier_semaphore()
    greeted = [(other, me) for other in others]
    greeted += [(ask_member[k], askers[k]) for k in range(groups)]
    greeted += [(member, partner) for member in range(groups)]
    for device in greeted:
        pl.semaphore_signal(barrier, inc=1, device_id=device, device_id_type=MESH)

    load = pltpu.make_async_copy(codes_ref, codes, load_sem)
    load_scales = pltpu.make_async_copy(scales_hbm, scales_ref, scales_sem)
    load_pairs = pltpu.make_async_copy(pairs_hbm, pairs_ref, pairs_sem)
    load_pairs.start()
    load_scales.start()
    load.start()
    load_pairs.wait()

    def slot_of(offset):
        slot = 0
        for s in range(groups):
            slot = slot + jnp.where(pairs_ref[1, s] // per_device == offset, s, 0)
        return slot

    def chosen(column, slot, side):
        return lax.rem(pairs_ref[side, groups * column + slot], per_device)

    my_rows = pl.ds(pl.multiple_of(dp * rows, rows), rows)
    right_pick = [chosen(askers[k], slot_of(order[k]), 1) for k in range(groups)]
    left_pick = [
        chosen(me, slot_of(pick(share_of(member, me), order)), 0) for member in others + [dp]
    ]
    load_scales.wait()
    factors = [scales_ref[:, expert, :].T for expert in range(per_device)]

    def scale_and_stage(c):
        for expert in range(per_device):
            for block in range(c * CHUNK // width, (c + 1) * CHUNK // width):
                at = slice(block * width, (block + 1) * width)
                inside = slice(block * width - c * CHUNK, (block + 1) * width - c * CHUNK)
                acts[expert, c, :, inside] = (
                    codes[expert, :, at].astype(jnp.float32) * factors[expert][:, block : block + 1]
                ).astype(jnp.bfloat16)
        for k in range(groups):
            send_right[k, c] = acts[right_pick[k], c]
        for r in range(groups - 1):
            send_left[r, c] = acts[left_pick[r], c]
        left_rows[c, my_rows, :] = acts[left_pick[-1], c]

    def left_copy(r, c):
        return pltpu.make_async_remote_copy(
            src_ref=send_left.at[r, c],
            dst_ref=left_rows.at[c, my_rows, :],
            send_sem=left_send_sem.at[r, c],
            recv_sem=left_sem.at[c, dp],
            device_id=(others[r], me),
            device_id_type=MESH,
        )

    def right_copy(k, c):
        return pltpu.make_async_remote_copy(
            src_ref=send_right.at[k, c],
            dst_ref=right_rows.at[c, my_rows, :],
            send_sem=right_send_sem.at[k, c],
            recv_sem=right_sem.at[c, dp],
            device_id=(ask_member[k], askers[k]),
            device_id_type=MESH,
        )

    load.wait()
    ahead = (2 * chunks + 2) // 3
    far_first = sorted(range(groups), key=lambda k: -min(order[k], n - order[k]))
    staged = 0
    for c in range(chunks):
        lefts = range(c * chunks // ahead, (c + 1) * chunks // ahead) if c < ahead else range(0)
        while staged <= max([c, *lefts]):
            scale_and_stage(staged)
            staged += 1
        if c == 0:
            pl.semaphore_wait(barrier, len(greeted))
        for k in far_first:
            right_copy(k, c).start()
        for at in lefts:
            for r in range(groups - 1):
                left_copy(r, at).start()

    best[...] = jnp.full_like(best, -jnp.inf)
    for i in range(chunks):
        at = slice(i * CHUNK, (i + 1) * CHUNK)
        for other in others:
            theirs = pl.ds(pl.multiple_of(other * rows, rows), rows)
            pltpu.make_async_remote_copy(
                src_ref=send_left.at[0, 0],
                dst_ref=left_rows.at[i, theirs, :],
                send_sem=left_send_sem.at[0, 0],
                recv_sem=left_sem.at[i, other],
                device_id=(other, me),
                device_id_type=MESH,
            ).wait_recv()
        block = left_rows[i]
        wide = block.astype(jnp.float32)
        square = jnp.sum(wide * wide, axis=0, keepdims=True) / all_rows
        inverse = 1.0 / jnp.sqrt(square + EPSILON)
        inv_left[at, :] = jnp.broadcast_to(inverse, (128, CHUNK)).T
        turned[at, :] = block.T

    def sent(c):
        for r in range(groups - 1):
            left_copy(r, c).wait_send()
        for k in range(groups):
            right_copy(k, c).wait_send()

    @pl.loop(0, chunks)
    def _(c):
        @pl.when(c >= 2)
        def _():
            sent(c - 2)

        for member in range(groups):
            pltpu.make_async_remote_copy(
                src_ref=send_right.at[0, 0],
                dst_ref=right_rows.at[c, pl.ds(member * rows, rows), :],
                send_sem=right_send_sem.at[0, 0],
                recv_sem=right_sem.at[c, member],
                device_id=(member, partner),
                device_id_type=MESH,
            ).wait_recv()
        block = right_rows[c]
        wide = block.astype(jnp.float32)
        square = jnp.sum(wide * wide, axis=0, keepdims=True) / all_rows
        inverse = 1.0 / jnp.sqrt(square + EPSILON)
        tops = [jnp.full((8, 128), -jnp.inf, jnp.float32) for _ in range(CHUNK // 128)]
        for i in range(chunks):
            at = slice(i * CHUNK, (i + 1) * CHUNK)
            gram = jnp.dot(turned[at, :], block, preferred_element_type=jnp.float32)
            scale = inv_left[at, :]
            running = best[at, :]
            for h in range(CHUNK // 128):
                lanes = slice(h * 128, (h + 1) * 128)
                scaled = gram[:, lanes] * scale
                running = jnp.maximum(running, scaled * inverse[:, lanes])
                gram_top = jnp.max(scaled.reshape(CHUNK // 8, 8, 128), axis=0)
                tops[h] = jnp.maximum(tops[h], gram_top)
            best[at, :] = running
        top = jnp.max(jnp.concatenate(tops, axis=1), axis=0, keepdims=True)
        right_row[c] = top * inverse / all_rows

    right_full = jnp.concatenate([right_row[c] for c in range(chunks)], axis=1)
    left_full = jnp.concatenate(
        [
            jnp.max(best[i * CHUNK : (i + 1) * CHUNK, :].T, axis=0, keepdims=True)
            for i in range(chunks)
        ],
        axis=1,
    ) / all_rows
    for member in range(groups):
        at = slice(member * part, (member + 1) * part)
        right_stage[member] = right_full[:, at]
        left_stage[member] = left_full[:, at]

    def right_result(member):
        return pltpu.make_async_remote_copy(
            src_ref=right_stage.at[member],
            dst_ref=right_got.at[mine],
            send_sem=out_send_sem.at[member],
            recv_sem=right_got_sem.at[mine],
            device_id=(member, partner),
            device_id_type=MESH,
        )

    def left_result(r):
        return pltpu.make_async_remote_copy(
            src_ref=left_stage.at[others[r]],
            dst_ref=left_got.at[mine],
            send_sem=out_send_sem.at[groups + r],
            recv_sem=left_got_sem.at[mine],
            device_id=(others[r], me),
            device_id_type=MESH,
        )

    for member in range(groups):
        right_result(member).start()
    for r in range(groups - 1):
        left_result(r).start()
    left_got[mine] = left_stage[dp]

    share_at = []
    for s in range(groups):
        offset = pairs_ref[1, s] // per_device
        share = 0
        for k in range(groups):
            share = share + jnp.where(offset == order[k], k, 0)
        share_at.append(share)

    for c in range(max(chunks - 2, 0), chunks):
        sent(c)

    for other in others:
        share = share_of(other, me)
        pltpu.make_async_remote_copy(
            src_ref=left_stage.at[0],
            dst_ref=left_got.at[share],
            send_sem=out_send_sem.at[0],
            recv_sem=left_got_sem.at[share],
            device_id=(other, me),
            device_id_type=MESH,
        ).wait_recv()
    for k in range(groups):
        pltpu.make_async_remote_copy(
            src_ref=right_stage.at[0],
            dst_ref=right_got.at[k],
            send_sem=out_send_sem.at[0],
            recv_sem=right_got_sem.at[k],
            device_id=(ask_member[k], askers[k]),
            device_id_type=MESH,
        ).wait_recv()
    for member in range(groups):
        right_result(member).wait_send()
    for r in range(groups - 1):
        left_result(r).wait_send()

    for s in range(groups):
        out_ref[s : s + 1, :] = left_got[share_at[s]]
        out_ref[groups + s : groups + s + 1, :] = right_got[share_at[s]]


def pair_call(order, turns, n, groups, collective_id, unit_codes, block_scales, pairs):
    per_device, rows, units = unit_codes.shape
    chunks = units // CHUNK
    part = units // groups
    out = jax.ShapeDtypeStruct((2 * groups, part), jnp.float32)
    anywhere = pl.BlockSpec(memory_space=pl.ANY)
    dma = pltpu.SemaphoreType.DMA
    return pl.pallas_call(
        functools.partial(pair_kernel, order, turns, n, groups),
        out_shape=out,
        in_specs=[anywhere, anywhere, anywhere],
        out_specs=pl.BlockSpec(memory_space=pltpu.VMEM),
        scratch_shapes=[
            pltpu.VMEM((block_scales.shape[1], per_device, rows), jnp.float32),
            pltpu.SMEM(pairs.shape, jnp.int32),
            pltpu.VMEM((per_device, rows, units), jnp.bfloat16),
            pltpu.VMEM((per_device, chunks, rows, CHUNK), jnp.bfloat16),
            pltpu.VMEM((groups - 1, chunks, rows, CHUNK), jnp.bfloat16),
            pltpu.VMEM((groups, chunks, rows, CHUNK), jnp.bfloat16),
            pltpu.VMEM((chunks, groups * rows, CHUNK), jnp.bfloat16),
            pltpu.VMEM((chunks, groups * rows, CHUNK), jnp.bfloat16),
            pltpu.VMEM((units, groups * rows), jnp.bfloat16),
            pltpu.VMEM((units, 128), jnp.float32),
            pltpu.VMEM((units, 128), jnp.float32),
            pltpu.VMEM((chunks, 1, CHUNK), jnp.float32),
            pltpu.VMEM((groups, 1, part), jnp.float32),
            pltpu.VMEM((groups, 1, part), jnp.float32),
            pltpu.VMEM((groups, 1, part), jnp.float32),
            pltpu.VMEM((groups, 1, part), jnp.float32),
            dma,
            dma,
            dma,
            dma((groups - 1, chunks)),
            dma((chunks, groups)),
            dma((groups, chunks)),
            dma((chunks, groups)),
            dma((2 * groups - 1,)),
            dma((groups,)),
            dma((groups,)),
        ],
        compiler_params=pltpu.CompilerParams(
            collective_id=collective_id, has_side_effects=True, vmem_limit_bytes=56 * 2**20
        ),
        cost_estimate=pl.CostEstimate(
            flops=2 * units * units * groups * rows, bytes_accessed=2 * units * rows * per_device, transcendentals=0
        ),
    )(unit_codes, jnp.transpose(block_scales, (1, 0, 2)), pairs)


def offset_sets(n, slots):
    fixed = sorted({1, n // 2, n - 1})
    rest = [o for o in range(1, n) if o not in fixed]
    free = slots - len(fixed)
    if free < 0 or math.comb(len(rest), free) > MAX_BRANCHES:
        return []
    return [tuple(sorted(fixed + list(more))) for more in itertools.combinations(rest, free)]


def body(unit_codes, block_scales, pair_list):
    n = lax.axis_size("expert")
    groups = lax.axis_size("dp")
    per_device, rows, units = unit_codes.shape
    slots = pair_list.shape[0] // n
    sets = offset_sets(n, slots)
    fits = (
        slots == groups
        and rows % 16 == 0
        and units % CHUNK == 0
        and CHUNK % (units // block_scales.shape[1]) == 0
        and units // block_scales.shape[1] % 128 == 0
        and units % (128 * groups) == 0
        and (groups * rows) % 128 == 0
    )
    if not sets or not fits:
        return general_body(unit_codes, block_scales, pair_list)
    columns = pair_list.T
    offsets = pair_list[:slots, 1] // per_device
    if slots == 4 and n > 4:
        free = [(sum(members) - 1 - n // 2 - (n - 1), at) for at, members in enumerate(sets)]
        side = lax.broadcasted_iota(jnp.int32, columns.shape, 0)
        slot = lax.broadcasted_iota(jnp.int32, columns.shape, 1)
        offsets = jnp.where((side == 1) & (slot < slots), columns // per_device, 0)
        branch = jnp.sum(sum(jnp.where(offsets == offset, at, 0) for offset, at in free))
        columns = jnp.where(side == 0, columns % per_device, columns)
        branch, columns = lax.optimization_barrier((branch, columns))
    else:
        branch = 0
        for at, members in enumerate(sets):
            same = jnp.all(jnp.any(offsets[:, None] == jnp.asarray(members)[None, :], axis=1))
            branch = branch + jnp.where(same, at, 0)
    calls = []
    for at, members in enumerate(sets):
        order, turns = TURNS.get(members, (members, (0,) * n)) if (n, groups) == (8, 4) else (members, (0,) * n)
        calls.append(functools.partial(pair_call, order, turns, n, groups, at))
    best = lax.switch(branch, calls, unit_codes, block_scales, columns)
    return (best[None, :slots], best[None, slots:])


def solution(mesh):
    in_specs = (P("expert", "dp", None), P("expert", None, "dp"), P())
    out_specs = (P("expert", None, "dp"), P("expert", None, "dp"))
    return jax.shard_map(body, mesh=mesh, in_specs=in_specs, out_specs=out_specs, check_vma=False)
```

```python
import functools
import itertools
import math

import jax
import jax.numpy as jnp
from jax import lax
from jax.experimental import pallas as pl
from jax.experimental.pallas import tpu as pltpu
from jax.sharding import PartitionSpec as P

EPSILON = 1e-06


def general_body(unit_codes, block_scales, pair_list):
    num_devices = lax.axis_size("expert")
    groups = lax.axis_size("dp")
    my_index = lax.axis_index("expert")
    dp_index = lax.axis_index("dp")
    per_device, row_count, unit_count = unit_codes.shape
    num_blocks = block_scales.shape[1]
    block_len = unit_count // num_blocks
    slice_width = unit_count // groups
    factor = jnp.transpose(block_scales, (0, 2, 1))[:, :, :, None]
    acts = (
        unit_codes.astype(jnp.float32).reshape(per_device, row_count, num_blocks, block_len)
        * factor
    )
    acts = acts.reshape(per_device, row_count, unit_count).astype(jnp.bfloat16)
    slot_count = pair_list.shape[0] // num_devices
    pair_table = pair_list.reshape(num_devices, slot_count, 2)
    my_pairs = lax.dynamic_index_in_dim(pair_table, my_index, 0, keepdims=False)
    left_local = my_pairs[:, 0] % per_device
    right_dev = my_pairs[:, 1] // per_device
    is_asked = pair_table[:, :, 1] // per_device == my_index
    chosen = jnp.sum(jnp.where(is_asked, pair_table[:, :, 1] % per_device, 0), axis=1)
    in_use = jnp.any(is_asked, axis=1)
    chooser = ((chosen[:, None] == jnp.arange(per_device)[None, :]) & in_use[:, None]).astype(
        jnp.bfloat16
    )
    own_full = lax.all_gather(acts, "dp", axis=1, tiled=True)
    flattened = acts.reshape(per_device, -1)
    outbound = jnp.dot(chooser, flattened, preferred_element_type=jnp.float32).astype(jnp.bfloat16)
    received = lax.all_to_all(
        outbound.reshape((num_devices,) + acts.shape[1:]),
        "expert",
        split_axis=0,
        concat_axis=0,
        tiled=True,
    )
    wanted = jnp.take(received, right_dev, axis=0)
    partner = lax.all_to_all(wanted, "dp", split_axis=2, concat_axis=1, tiled=True)
    all_rows = partner.shape[1]
    own_square = (
        jnp.einsum("era,era->ea", own_full, own_full, preferred_element_type=jnp.float32) / all_rows
    )
    inv_own = 1.0 / jnp.sqrt(own_square + EPSILON)
    part_square = (
        jnp.einsum("srb,srb->sb", partner, partner, preferred_element_type=jnp.float32) / all_rows
    )
    inv_part = 1.0 / jnp.sqrt(part_square + EPSILON)

    def single(member):
        expert_pick, partner_block, inv_unit = member
        left_rows = jnp.take(own_full, expert_pick, axis=0)
        gram_block = jnp.einsum(
            "ra,rb->ab", left_rows, partner_block, preferred_element_type=jnp.float32
        )
        correlation = (
            gram_block
            / all_rows
            * jnp.take(inv_own, expert_pick, axis=0)[:, None]
            * inv_unit[None, :]
        )
        return (jnp.max(correlation, axis=1), jnp.max(correlation, axis=0))

    def several(member):
        return jax.vmap(single)(member)

    bundle = math.gcd(slot_count, 4)
    stacked = (
        left_local.reshape(-1, bundle),
        partner.reshape(-1, bundle, all_rows, slice_width),
        inv_part.reshape(-1, bundle, slice_width),
    )
    left_part, right_part = lax.map(several, stacked)
    left_part = left_part.reshape(slot_count, unit_count)
    right_part = right_part.reshape(slot_count, slice_width)
    left_all = lax.pmax(left_part, "dp")
    left_out = lax.dynamic_slice_in_dim(left_all, dp_index * slice_width, slice_width, 1)
    target = (right_dev[:, None] == jnp.arange(num_devices)[None, :]).astype(jnp.float32)
    outgoing = jnp.dot(
        target.T, right_part, precision=lax.Precision.HIGHEST, preferred_element_type=jnp.float32
    )
    returned = lax.all_to_all(outgoing, "expert", split_axis=0, concat_axis=0, tiled=True)
    offsets = pair_table[0, :, 1] // per_device
    source_dev = (my_index - offsets) % num_devices
    right_out = jnp.take(returned, source_dev, axis=0)
    return (left_out[None], right_out[None])


MESH = pl.DeviceIdType.MESH
CHUNK = 256
MAX_BRANCHES = 8
TURNS = {
    (1, 2, 4, 7): ((1, 7, 4, 2), (1, 1, 2, 2, 0, 3, 1, 0)),
    (1, 3, 4, 7): ((1, 4, 7, 3), (0, 1, 3, 0, 3, 1, 2, 0)),
    (1, 4, 5, 7): ((1, 4, 7, 5), (0, 0, 1, 3, 3, 2, 1, 2)),
    (1, 4, 6, 7): ((1, 7, 6, 4), (0, 2, 1, 3, 2, 3, 3, 0)),
}


def pick(index, table):
    total = 0
    size = len(table)
    for at, value in enumerate(table):
        if value:
            apart = (index - at) * (index - at)
            total = total + value * (1 - (apart + size * size - 1) // (size * size))
    return total


def pair_kernel(
    order, turns, n, groups,
    codes_ref, scales_hbm, pairs_hbm, out_ref,
    scales_ref, pairs_ref, codes, acts, send_left, send_right, left_rows, right_rows, turned, inv_left, best, right_row,
    left_stage, right_stage, left_got, right_got,
    load_sem, scales_sem, pairs_sem, left_send_sem, left_sem, right_send_sem, right_sem, out_send_sem, left_got_sem, right_got_sem,
):
    me = lax.axis_index("expert")
    dp = lax.axis_index("dp")
    per_device, rows, units = codes_ref.shape
    blocks = scales_hbm.shape[0]
    width = units // blocks
    chunks = units // CHUNK
    part = units // groups
    all_rows = groups * rows

    def share_of(member, column):
        return (member - pick(column, turns) + groups) % groups

    def member_of(share, column):
        return (share + pick(column, turns)) % groups

    mine = share_of(dp, me)
    my_offset = pick(mine, order)
    partner = (me + my_offset) % n
    askers = [(me - order[k] + n) % n for k in range(groups)]
    ask_member = [member_of(k, askers[k]) for k in range(groups)]
    others = [(dp + r) % groups for r in range(1, groups)]
    far_first = sorted(range(groups), key=lambda k: -min(order[k], n - order[k]))

    load = pltpu.make_async_copy(codes_ref, codes, load_sem)
    load_scales = pltpu.make_async_copy(scales_hbm, scales_ref, scales_sem)
    load_pairs = pltpu.make_async_copy(pairs_hbm, pairs_ref, pairs_sem)
    load_pairs.start()
    load_scales.start()
    load.start()

    barrier = pltpu.get_barrier_semaphore()
    greeted = [(ask_member[k], askers[k]) for k in far_first]
    greeted += [(member, partner) for member in range(groups)]
    greeted += [(other, me) for other in others]
    for device in greeted:
        pl.semaphore_signal(barrier, inc=1, device_id=device, device_id_type=MESH)

    load_pairs.wait()

    def slot_of(offset):
        slot = 0
        for s in range(groups):
            slot = slot + jnp.where(pairs_ref[1, s] // per_device == offset, s, 0)
        return slot

    def chosen(column, slot, side):
        return lax.rem(pairs_ref[side, groups * column + slot], per_device)

    my_rows = pl.ds(pl.multiple_of(dp * rows, rows), rows)
    right_pick = [chosen(askers[k], slot_of(order[k]), 1) for k in range(groups)]
    left_pick = [
        chosen(me, slot_of(pick(share_of(member, me), order)), 0) for member in others + [dp]
    ]
    load_scales.wait()
    factors = [scales_ref[:, expert, :].T for expert in range(per_device)]

    def scale_and_stage(c):
        for expert in range(per_device):
            for block in range(c * CHUNK // width, (c + 1) * CHUNK // width):
                at = slice(block * width, (block + 1) * width)
                inside = slice(block * width - c * CHUNK, (block + 1) * width - c * CHUNK)
                acts[expert, c, :, inside] = (
                    codes[expert, :, at].astype(jnp.float32) * factors[expert][:, block : block + 1]
                ).astype(jnp.bfloat16)
        for k in range(groups):
            send_right[k, c] = acts[right_pick[k], c]
        for r in range(groups - 1):
            send_left[r, c] = acts[left_pick[r], c]
        left_rows[c, my_rows, :] = acts[left_pick[-1], c]

    def left_copy(r, c):
        return pltpu.make_async_remote_copy(
            src_ref=send_left.at[r, c],
            dst_ref=left_rows.at[c, my_rows, :],
            send_sem=left_send_sem.at[r, c],
            recv_sem=left_sem.at[c, dp],
            device_id=(others[r], me),
            device_id_type=MESH,
        )

    def right_copy(k, c):
        return pltpu.make_async_remote_copy(
            src_ref=send_right.at[k, c],
            dst_ref=right_rows.at[c, my_rows, :],
            send_sem=right_send_sem.at[k, c],
            recv_sem=right_sem.at[c, dp],
            device_id=(ask_member[k], askers[k]),
            device_id_type=MESH,
        )

    load.wait()
    ahead = (2 * chunks + 2) // 3
    staged = 0
    for c in range(chunks):
        lefts = range(c * chunks // ahead, (c + 1) * chunks // ahead) if c < ahead else range(0)
        while staged <= max([c, *lefts]):
            scale_and_stage(staged)
            staged += 1
        if c == 0:
            pl.semaphore_wait(barrier, len(greeted))
        for k in far_first:
            right_copy(k, c).start()
        for at in lefts:
            for r in range(groups - 1):
                left_copy(r, at).start()

    best[...] = jnp.full_like(best, -jnp.inf)
    for i in range(chunks):
        at = slice(i * CHUNK, (i + 1) * CHUNK)
        for other in others:
            theirs = pl.ds(pl.multiple_of(other * rows, rows), rows)
            pltpu.make_async_remote_copy(
                src_ref=send_left.at[0, 0],
                dst_ref=left_rows.at[i, theirs, :],
                send_sem=left_send_sem.at[0, 0],
                recv_sem=left_sem.at[i, other],
                device_id=(other, me),
                device_id_type=MESH,
            ).wait_recv()
        block = left_rows[i]
        wide = block.astype(jnp.float32)
        square = jnp.sum(wide * wide, axis=0, keepdims=True) / all_rows
        inverse = 1.0 / jnp.sqrt(square + EPSILON)
        inv_left[at, :] = jnp.broadcast_to(inverse, (128, CHUNK)).T
        turned[at, :] = block.T

    def sent(c):
        for r in range(groups - 1):
            left_copy(r, c).wait_send()
        for k in range(groups):
            right_copy(k, c).wait_send()

    @pl.loop(0, chunks)
    def _(c):
        @pl.when(c >= 2)
        def _():
            sent(c - 2)

        for member in range(groups):
            pltpu.make_async_remote_copy(
                src_ref=send_right.at[0, 0],
                dst_ref=right_rows.at[c, pl.ds(member * rows, rows), :],
                send_sem=right_send_sem.at[0, 0],
                recv_sem=right_sem.at[c, member],
                device_id=(member, partner),
                device_id_type=MESH,
            ).wait_recv()
        block = right_rows[c]
        wide = block.astype(jnp.float32)
        square = jnp.sum(wide * wide, axis=0, keepdims=True) / all_rows
        inverse = 1.0 / jnp.sqrt(square + EPSILON)
        tops = [jnp.full((8, 128), -jnp.inf, jnp.float32) for _ in range(CHUNK // 128)]
        for i in range(chunks):
            at = slice(i * CHUNK, (i + 1) * CHUNK)
            gram = jnp.dot(turned[at, :], block, preferred_element_type=jnp.float32)
            scale = inv_left[at, :]
            running = best[at, :]
            for h in range(CHUNK // 128):
                lanes = slice(h * 128, (h + 1) * 128)
                scaled = gram[:, lanes] * scale
                running = jnp.maximum(running, scaled * inverse[:, lanes])
                gram_top = jnp.max(scaled.reshape(CHUNK // 8, 8, 128), axis=0)
                tops[h] = jnp.maximum(tops[h], gram_top)
            best[at, :] = running
        top = jnp.max(jnp.concatenate(tops, axis=1), axis=0, keepdims=True)
        right_row[c] = top * inverse / all_rows

    right_full = jnp.concatenate([right_row[c] for c in range(chunks)], axis=1)
    left_full = jnp.concatenate(
        [
            jnp.max(best[i * CHUNK : (i + 1) * CHUNK, :].T, axis=0, keepdims=True)
            for i in range(chunks)
        ],
        axis=1,
    ) / all_rows
    for member in range(groups):
        at = slice(member * part, (member + 1) * part)
        right_stage[member] = right_full[:, at]
        left_stage[member] = left_full[:, at]

    def right_result(member):
        return pltpu.make_async_remote_copy(
            src_ref=right_stage.at[member],
            dst_ref=right_got.at[mine],
            send_sem=out_send_sem.at[member],
            recv_sem=right_got_sem.at[mine],
            device_id=(member, partner),
            device_id_type=MESH,
        )

    def left_result(r):
        return pltpu.make_async_remote_copy(
            src_ref=left_stage.at[others[r]],
            dst_ref=left_got.at[mine],
            send_sem=out_send_sem.at[groups + r],
            recv_sem=left_got_sem.at[mine],
            device_id=(others[r], me),
            device_id_type=MESH,
        )

    for member in range(groups):
        right_result(member).start()
    for r in range(groups - 1):
        left_result(r).start()
    left_got[mine] = left_stage[dp]

    share_at = []
    for s in range(groups):
        offset = pairs_ref[1, s] // per_device
        share = 0
        for k in range(groups):
            share = share + jnp.where(offset == order[k], k, 0)
        share_at.append(share)

    for c in range(max(chunks - 2, 0), chunks):
        sent(c)

    for other in others:
        share = share_of(other, me)
        pltpu.make_async_remote_copy(
            src_ref=left_stage.at[0],
            dst_ref=left_got.at[share],
            send_sem=out_send_sem.at[0],
            recv_sem=left_got_sem.at[share],
            device_id=(other, me),
            device_id_type=MESH,
        ).wait_recv()
    for k in range(groups):
        pltpu.make_async_remote_copy(
            src_ref=right_stage.at[0],
            dst_ref=right_got.at[k],
            send_sem=out_send_sem.at[0],
            recv_sem=right_got_sem.at[k],
            device_id=(ask_member[k], askers[k]),
            device_id_type=MESH,
        ).wait_recv()
    for member in range(groups):
        right_result(member).wait_send()
    for r in range(groups - 1):
        left_result(r).wait_send()

    for s in range(groups):
        out_ref[s : s + 1, :] = left_got[share_at[s]]
        out_ref[groups + s : groups + s + 1, :] = right_got[share_at[s]]


def pair_call(order, turns, n, groups, collective_id, unit_codes, block_scales, pairs):
    per_device, rows, units = unit_codes.shape
    chunks = units // CHUNK
    part = units // groups
    out = jax.ShapeDtypeStruct((2 * groups, part), jnp.float32)
    anywhere = pl.BlockSpec(memory_space=pl.ANY)
    dma = pltpu.SemaphoreType.DMA
    return pl.pallas_call(
        functools.partial(pair_kernel, order, turns, n, groups),
        out_shape=out,
        in_specs=[anywhere, anywhere, anywhere],
        out_specs=pl.BlockSpec(memory_space=pltpu.VMEM),
        scratch_shapes=[
            pltpu.VMEM((block_scales.shape[1], per_device, rows), jnp.float32),
            pltpu.SMEM(pairs.shape, jnp.int32),
            pltpu.VMEM((per_device, rows, units), jnp.bfloat16),
            pltpu.VMEM((per_device, chunks, rows, CHUNK), jnp.bfloat16),
            pltpu.VMEM((groups - 1, chunks, rows, CHUNK), jnp.bfloat16),
            pltpu.VMEM((groups, chunks, rows, CHUNK), jnp.bfloat16),
            pltpu.VMEM((chunks, groups * rows, CHUNK), jnp.bfloat16),
            pltpu.VMEM((chunks, groups * rows, CHUNK), jnp.bfloat16),
            pltpu.VMEM((units, groups * rows), jnp.bfloat16),
            pltpu.VMEM((units, 128), jnp.float32),
            pltpu.VMEM((units, 128), jnp.float32),
            pltpu.VMEM((chunks, 1, CHUNK), jnp.float32),
            pltpu.VMEM((groups, 1, part), jnp.float32),
            pltpu.VMEM((groups, 1, part), jnp.float32),
            pltpu.VMEM((groups, 1, part), jnp.float32),
            pltpu.VMEM((groups, 1, part), jnp.float32),
            dma,
            dma,
            dma,
            dma((groups - 1, chunks)),
            dma((chunks, groups)),
            dma((groups, chunks)),
            dma((chunks, groups)),
            dma((2 * groups - 1,)),
            dma((groups,)),
            dma((groups,)),
        ],
        compiler_params=pltpu.CompilerParams(
            collective_id=collective_id, has_side_effects=True, vmem_limit_bytes=56 * 2**20
        ),
        cost_estimate=pl.CostEstimate(
            flops=2 * units * units * groups * rows, bytes_accessed=2 * units * rows * per_device, transcendentals=0
        ),
    )(unit_codes, jnp.transpose(block_scales, (1, 0, 2)), pairs)


def offset_sets(n, slots):
    fixed = sorted({1, n // 2, n - 1})
    rest = [o for o in range(1, n) if o not in fixed]
    free = slots - len(fixed)
    if free < 0 or math.comb(len(rest), free) > MAX_BRANCHES:
        return []
    return [tuple(sorted(fixed + list(more))) for more in itertools.combinations(rest, free)]


def body(unit_codes, block_scales, pair_list):
    n = lax.axis_size("expert")
    groups = lax.axis_size("dp")
    per_device, rows, units = unit_codes.shape
    slots = pair_list.shape[0] // n
    sets = offset_sets(n, slots)
    fits = (
        slots == groups
        and rows % 16 == 0
        and units % CHUNK == 0
        and CHUNK % (units // block_scales.shape[1]) == 0
        and units // block_scales.shape[1] % 128 == 0
        and units % (128 * groups) == 0
        and (groups * rows) % 128 == 0
    )
    if not sets or not fits:
        return general_body(unit_codes, block_scales, pair_list)
    columns = pair_list.T
    offsets = pair_list[:slots, 1] // per_device
    if slots == 4 and n > 4:
        free = [(sum(members) - 1 - n // 2 - (n - 1), at) for at, members in enumerate(sets)]
        side = lax.broadcasted_iota(jnp.int32, columns.shape, 0)
        slot = lax.broadcasted_iota(jnp.int32, columns.shape, 1)
        offsets = jnp.where((side == 1) & (slot < slots), columns // per_device, 0)
        branch = jnp.sum(sum(jnp.where(offsets == offset, at, 0) for offset, at in free))
        columns = jnp.where(side == 0, columns % per_device, columns)
        branch, columns = lax.optimization_barrier((branch, columns))
    else:
        branch = 0
        for at, members in enumerate(sets):
            same = jnp.all(jnp.any(offsets[:, None] == jnp.asarray(members)[None, :], axis=1))
            branch = branch + jnp.where(same, at, 0)
    calls = []
    for at, members in enumerate(sets):
        order, turns = TURNS.get(members, (members, (0,) * n)) if (n, groups) == (8, 4) else (members, (0,) * n)
        calls.append(functools.partial(pair_call, order, turns, n, groups, at))
    best = lax.switch(branch, calls, unit_codes, block_scales, columns)
    return (best[None, :slots], best[None, slots:])


def solution(mesh):
    in_specs = (P("expert", "dp", None), P("expert", None, "dp"), P())
    out_specs = (P("expert", None, "dp"), P("expert", None, "dp"))
    return jax.shard_map(body, mesh=mesh, in_specs=in_specs, out_specs=out_specs, check_vma=False)
```

```python
import functools
import itertools
import math

import jax
import jax.numpy as jnp
from jax import lax
from jax.experimental import pallas as pl
from jax.experimental.pallas import tpu as pltpu
from jax.sharding import PartitionSpec as P

EPSILON = 1e-06


def general_body(unit_codes, block_scales, pair_list):
    num_devices = lax.axis_size("expert")
    groups = lax.axis_size("dp")
    my_index = lax.axis_index("expert")
    dp_index = lax.axis_index("dp")
    per_device, row_count, unit_count = unit_codes.shape
    num_blocks = block_scales.shape[1]
    block_len = unit_count // num_blocks
    slice_width = unit_count // groups
    factor = jnp.transpose(block_scales, (0, 2, 1))[:, :, :, None]
    acts = (
        unit_codes.astype(jnp.float32).reshape(per_device, row_count, num_blocks, block_len)
        * factor
    )
    acts = acts.reshape(per_device, row_count, unit_count).astype(jnp.bfloat16)
    slot_count = pair_list.shape[0] // num_devices
    pair_table = pair_list.reshape(num_devices, slot_count, 2)
    my_pairs = lax.dynamic_index_in_dim(pair_table, my_index, 0, keepdims=False)
    left_local = my_pairs[:, 0] % per_device
    right_dev = my_pairs[:, 1] // per_device
    is_asked = pair_table[:, :, 1] // per_device == my_index
    chosen = jnp.sum(jnp.where(is_asked, pair_table[:, :, 1] % per_device, 0), axis=1)
    in_use = jnp.any(is_asked, axis=1)
    chooser = ((chosen[:, None] == jnp.arange(per_device)[None, :]) & in_use[:, None]).astype(
        jnp.bfloat16
    )
    own_full = lax.all_gather(acts, "dp", axis=1, tiled=True)
    flattened = acts.reshape(per_device, -1)
    outbound = jnp.dot(chooser, flattened, preferred_element_type=jnp.float32).astype(jnp.bfloat16)
    received = lax.all_to_all(
        outbound.reshape((num_devices,) + acts.shape[1:]),
        "expert",
        split_axis=0,
        concat_axis=0,
        tiled=True,
    )
    wanted = jnp.take(received, right_dev, axis=0)
    partner = lax.all_to_all(wanted, "dp", split_axis=2, concat_axis=1, tiled=True)
    all_rows = partner.shape[1]
    own_square = (
        jnp.einsum("era,era->ea", own_full, own_full, preferred_element_type=jnp.float32) / all_rows
    )
    inv_own = 1.0 / jnp.sqrt(own_square + EPSILON)
    part_square = (
        jnp.einsum("srb,srb->sb", partner, partner, preferred_element_type=jnp.float32) / all_rows
    )
    inv_part = 1.0 / jnp.sqrt(part_square + EPSILON)

    def single(member):
        expert_pick, partner_block, inv_unit = member
        left_rows = jnp.take(own_full, expert_pick, axis=0)
        gram_block = jnp.einsum(
            "ra,rb->ab", left_rows, partner_block, preferred_element_type=jnp.float32
        )
        correlation = (
            gram_block
            / all_rows
            * jnp.take(inv_own, expert_pick, axis=0)[:, None]
            * inv_unit[None, :]
        )
        return (jnp.max(correlation, axis=1), jnp.max(correlation, axis=0))

    def several(member):
        return jax.vmap(single)(member)

    bundle = math.gcd(slot_count, 4)
    stacked = (
        left_local.reshape(-1, bundle),
        partner.reshape(-1, bundle, all_rows, slice_width),
        inv_part.reshape(-1, bundle, slice_width),
    )
    left_part, right_part = lax.map(several, stacked)
    left_part = left_part.reshape(slot_count, unit_count)
    right_part = right_part.reshape(slot_count, slice_width)
    left_all = lax.pmax(left_part, "dp")
    left_out = lax.dynamic_slice_in_dim(left_all, dp_index * slice_width, slice_width, 1)
    target = (right_dev[:, None] == jnp.arange(num_devices)[None, :]).astype(jnp.float32)
    outgoing = jnp.dot(
        target.T, right_part, precision=lax.Precision.HIGHEST, preferred_element_type=jnp.float32
    )
    returned = lax.all_to_all(outgoing, "expert", split_axis=0, concat_axis=0, tiled=True)
    offsets = pair_table[0, :, 1] // per_device
    source_dev = (my_index - offsets) % num_devices
    right_out = jnp.take(returned, source_dev, axis=0)
    return (left_out[None], right_out[None])


MESH = pl.DeviceIdType.MESH
CHUNK = 256
MAX_BRANCHES = 8
TURNS = {
    (1, 2, 4, 7): ((7, 1, 2, 4), (0, 3, 3, 2, 3, 1, 2, 0)),
    (1, 3, 4, 7): ((1, 4, 7, 3), (0, 1, 3, 0, 3, 1, 2, 0)),
    (1, 4, 5, 7): ((1, 4, 7, 5), (0, 0, 1, 3, 3, 2, 1, 2)),
    (1, 4, 6, 7): ((1, 7, 6, 4), (0, 2, 1, 3, 2, 3, 3, 0)),
}


def pick(index, table):
    total = 0
    size = len(table)
    for at, value in enumerate(table):
        if value:
            apart = (index - at) * (index - at)
            total = total + value * (1 - (apart + size * size - 1) // (size * size))
    return total


def pair_kernel(
    order, turns, n, groups,
    codes_ref, scales_hbm, pairs_hbm, out_ref,
    scales_ref, pairs_ref, codes, acts, send_left, send_right, left_rows, right_rows, turned, inv_left, best, right_row,
    left_stage, right_stage, left_got, right_got,
    load_sem, scales_sem, pairs_sem, left_send_sem, left_sem, right_send_sem, right_sem, out_send_sem, left_got_sem, right_got_sem,
):
    me = lax.axis_index("expert")
    dp = lax.axis_index("dp")
    per_device, rows, units = codes_ref.shape
    blocks = scales_hbm.shape[0]
    width = units // blocks
    chunks = units // CHUNK
    part = units // groups
    all_rows = groups * rows

    def share_of(member, column):
        return (member - pick(column, turns) + groups) % groups

    def member_of(share, column):
        return (share + pick(column, turns)) % groups

    mine = share_of(dp, me)
    my_offset = pick(mine, order)
    partner = (me + my_offset) % n
    askers = [(me - order[k] + n) % n for k in range(groups)]
    ask_member = [member_of(k, askers[k]) for k in range(groups)]
    others = [(dp + r) % groups for r in range(1, groups)]
    far_first = sorted(range(groups), key=lambda k: -min(order[k], n - order[k]))

    load = pltpu.make_async_copy(codes_ref, codes, load_sem)
    load_scales = pltpu.make_async_copy(scales_hbm, scales_ref, scales_sem)
    load_pairs = pltpu.make_async_copy(pairs_hbm, pairs_ref, pairs_sem)
    load_pairs.start()
    load_scales.start()
    load.start()

    barrier = pltpu.get_barrier_semaphore()
    greeted = [(ask_member[k], askers[k]) for k in far_first]
    greeted += [(member, partner) for member in range(groups)]
    greeted += [(other, me) for other in others]
    for device in greeted:
        pl.semaphore_signal(barrier, inc=1, device_id=device, device_id_type=MESH)

    load_pairs.wait()

    def slot_of(offset):
        slot = 0
        for s in range(groups):
            slot = slot + jnp.where(pairs_ref[1, s] // per_device == offset, s, 0)
        return slot

    def chosen(column, slot, side):
        return lax.rem(pairs_ref[side, groups * column + slot], per_device)

    my_rows = pl.ds(pl.multiple_of(dp * rows, rows), rows)
    right_pick = [chosen(askers[k], slot_of(order[k]), 1) for k in range(groups)]
    left_pick = [
        chosen(me, slot_of(pick(share_of(member, me), order)), 0) for member in others + [dp]
    ]
    load_scales.wait()
    factors = [scales_ref[:, expert, :].T for expert in range(per_device)]

    def scale_and_stage(c):
        for expert in range(per_device):
            for block in range(c * CHUNK // width, (c + 1) * CHUNK // width):
                at = slice(block * width, (block + 1) * width)
                inside = slice(block * width - c * CHUNK, (block + 1) * width - c * CHUNK)
                acts[expert, c, :, inside] = (
                    codes[expert, :, at].astype(jnp.float32) * factors[expert][:, block : block + 1]
                ).astype(jnp.bfloat16)
        for k in range(groups):
            send_right[k, c] = acts[right_pick[k], c]
        for r in range(groups - 1):
            send_left[r, c] = acts[left_pick[r], c]
        left_rows[c, my_rows, :] = acts[left_pick[-1], c]

    def left_copy(r, c):
        return pltpu.make_async_remote_copy(
            src_ref=send_left.at[r, c],
            dst_ref=left_rows.at[c, my_rows, :],
            send_sem=left_send_sem.at[r, c],
            recv_sem=left_sem.at[c, dp],
            device_id=(others[r], me),
            device_id_type=MESH,
        )

    def right_copy(k, c):
        return pltpu.make_async_remote_copy(
            src_ref=send_right.at[k, c],
            dst_ref=right_rows.at[c, my_rows, :],
            send_sem=right_send_sem.at[k, c],
            recv_sem=right_sem.at[c, dp],
            device_id=(ask_member[k], askers[k]),
            device_id_type=MESH,
        )

    load.wait()
    ahead = (2 * chunks + 2) // 3
    staged = 0
    for c in range(chunks):
        lefts = range(c * chunks // ahead, (c + 1) * chunks // ahead) if c < ahead else range(0)
        while staged <= max([c, *lefts]):
            scale_and_stage(staged)
            staged += 1
        if c == 0:
            pl.semaphore_wait(barrier, len(greeted))
        for k in far_first:
            right_copy(k, c).start()
        for at in lefts:
            for r in range(groups - 1):
                left_copy(r, at).start()

    best[...] = jnp.full_like(best, -jnp.inf)
    for i in range(chunks):
        at = slice(i * CHUNK, (i + 1) * CHUNK)
        for other in others:
            theirs = pl.ds(pl.multiple_of(other * rows, rows), rows)
            pltpu.make_async_remote_copy(
                src_ref=send_left.at[0, 0],
                dst_ref=left_rows.at[i, theirs, :],
                send_sem=left_send_sem.at[0, 0],
                recv_sem=left_sem.at[i, other],
                device_id=(other, me),
                device_id_type=MESH,
            ).wait_recv()
        block = left_rows[i]
        wide = block.astype(jnp.float32)
        square = jnp.sum(wide * wide, axis=0, keepdims=True) / all_rows
        inverse = 1.0 / jnp.sqrt(square + EPSILON)
        inv_left[at, :] = jnp.broadcast_to(inverse, (128, CHUNK)).T
        turned[at, :] = block.T

    def sent(c):
        for r in range(groups - 1):
            left_copy(r, c).wait_send()
        for k in range(groups):
            right_copy(k, c).wait_send()

    @pl.loop(0, chunks)
    def _(c):
        @pl.when(c >= 2)
        def _():
            sent(c - 2)

        for member in range(groups):
            pltpu.make_async_remote_copy(
                src_ref=send_right.at[0, 0],
                dst_ref=right_rows.at[c, pl.ds(member * rows, rows), :],
                send_sem=right_send_sem.at[0, 0],
                recv_sem=right_sem.at[c, member],
                device_id=(member, partner),
                device_id_type=MESH,
            ).wait_recv()
        block = right_rows[c]
        wide = block.astype(jnp.float32)
        square = jnp.sum(wide * wide, axis=0, keepdims=True) / all_rows
        inverse = 1.0 / jnp.sqrt(square + EPSILON)
        tops = [jnp.full((8, 128), -jnp.inf, jnp.float32) for _ in range(CHUNK // 128)]
        for i in range(chunks):
            at = slice(i * CHUNK, (i + 1) * CHUNK)
            gram = jnp.dot(turned[at, :], block, preferred_element_type=jnp.float32)
            scale = inv_left[at, :]
            running = best[at, :]
            for h in range(CHUNK // 128):
                lanes = slice(h * 128, (h + 1) * 128)
                scaled = gram[:, lanes] * scale
                running = jnp.maximum(running, scaled * inverse[:, lanes])
                gram_top = jnp.max(scaled.reshape(CHUNK // 8, 8, 128), axis=0)
                tops[h] = jnp.maximum(tops[h], gram_top)
            best[at, :] = running
        top = jnp.max(jnp.concatenate(tops, axis=1), axis=0, keepdims=True)
        right_row[c] = top * inverse / all_rows

    right_full = jnp.concatenate([right_row[c] for c in range(chunks)], axis=1)
    left_full = jnp.concatenate(
        [
            jnp.max(best[i * CHUNK : (i + 1) * CHUNK, :].T, axis=0, keepdims=True)
            for i in range(chunks)
        ],
        axis=1,
    ) / all_rows
    for member in range(groups):
        at = slice(member * part, (member + 1) * part)
        right_stage[member] = right_full[:, at]
        left_stage[member] = left_full[:, at]

    def right_result(member):
        return pltpu.make_async_remote_copy(
            src_ref=right_stage.at[member],
            dst_ref=right_got.at[mine],
            send_sem=out_send_sem.at[member],
            recv_sem=right_got_sem.at[mine],
            device_id=(member, partner),
            device_id_type=MESH,
        )

    def left_result(r):
        return pltpu.make_async_remote_copy(
            src_ref=left_stage.at[others[r]],
            dst_ref=left_got.at[mine],
            send_sem=out_send_sem.at[groups + r],
            recv_sem=left_got_sem.at[mine],
            device_id=(others[r], me),
            device_id_type=MESH,
        )

    for member in range(groups):
        right_result(member).start()
    for r in range(groups - 1):
        left_result(r).start()
    left_got[mine] = left_stage[dp]

    share_at = []
    for s in range(groups):
        offset = pairs_ref[1, s] // per_device
        share = 0
        for k in range(groups):
            share = share + jnp.where(offset == order[k], k, 0)
        share_at.append(share)

    for c in range(max(chunks - 2, 0), chunks):
        sent(c)

    for other in others:
        share = share_of(other, me)
        pltpu.make_async_remote_copy(
            src_ref=left_stage.at[0],
            dst_ref=left_got.at[share],
            send_sem=out_send_sem.at[0],
            recv_sem=left_got_sem.at[share],
            device_id=(other, me),
            device_id_type=MESH,
        ).wait_recv()
    for k in range(groups):
        pltpu.make_async_remote_copy(
            src_ref=right_stage.at[0],
            dst_ref=right_got.at[k],
            send_sem=out_send_sem.at[0],
            recv_sem=right_got_sem.at[k],
            device_id=(ask_member[k], askers[k]),
            device_id_type=MESH,
        ).wait_recv()
    for member in range(groups):
        right_result(member).wait_send()
    for r in range(groups - 1):
        left_result(r).wait_send()

    for s in range(groups):
        out_ref[s : s + 1, :] = left_got[share_at[s]]
        out_ref[groups + s : groups + s + 1, :] = right_got[share_at[s]]


def pair_call(order, turns, n, groups, collective_id, unit_codes, block_scales, pairs):
    per_device, rows, units = unit_codes.shape
    chunks = units // CHUNK
    part = units // groups
    out = jax.ShapeDtypeStruct((2 * groups, part), jnp.float32)
    anywhere = pl.BlockSpec(memory_space=pl.ANY)
    dma = pltpu.SemaphoreType.DMA
    return pl.pallas_call(
        functools.partial(pair_kernel, order, turns, n, groups),
        out_shape=out,
        in_specs=[anywhere, anywhere, anywhere],
        out_specs=pl.BlockSpec(memory_space=pltpu.VMEM),
        scratch_shapes=[
            pltpu.VMEM((block_scales.shape[1], per_device, rows), jnp.float32),
            pltpu.SMEM(pairs.shape, jnp.int32),
            pltpu.VMEM((per_device, rows, units), jnp.bfloat16),
            pltpu.VMEM((per_device, chunks, rows, CHUNK), jnp.bfloat16),
            pltpu.VMEM((groups - 1, chunks, rows, CHUNK), jnp.bfloat16),
            pltpu.VMEM((groups, chunks, rows, CHUNK), jnp.bfloat16),
            pltpu.VMEM((chunks, groups * rows, CHUNK), jnp.bfloat16),
            pltpu.VMEM((chunks, groups * rows, CHUNK), jnp.bfloat16),
            pltpu.VMEM((units, groups * rows), jnp.bfloat16),
            pltpu.VMEM((units, 128), jnp.float32),
            pltpu.VMEM((units, 128), jnp.float32),
            pltpu.VMEM((chunks, 1, CHUNK), jnp.float32),
            pltpu.VMEM((groups, 1, part), jnp.float32),
            pltpu.VMEM((groups, 1, part), jnp.float32),
            pltpu.VMEM((groups, 1, part), jnp.float32),
            pltpu.VMEM((groups, 1, part), jnp.float32),
            dma,
            dma,
            dma,
            dma((groups - 1, chunks)),
            dma((chunks, groups)),
            dma((groups, chunks)),
            dma((chunks, groups)),
            dma((2 * groups - 1,)),
            dma((groups,)),
            dma((groups,)),
        ],
        compiler_params=pltpu.CompilerParams(
            collective_id=collective_id, has_side_effects=True, vmem_limit_bytes=56 * 2**20
        ),
        cost_estimate=pl.CostEstimate(
            flops=2 * units * units * groups * rows, bytes_accessed=2 * units * rows * per_device, transcendentals=0
        ),
    )(unit_codes, jnp.transpose(block_scales, (1, 0, 2)), pairs)


def offset_sets(n, slots):
    fixed = sorted({1, n // 2, n - 1})
    rest = [o for o in range(1, n) if o not in fixed]
    free = slots - len(fixed)
    if free < 0 or math.comb(len(rest), free) > MAX_BRANCHES:
        return []
    return [tuple(sorted(fixed + list(more))) for more in itertools.combinations(rest, free)]


def body(unit_codes, block_scales, pair_list):
    n = lax.axis_size("expert")
    groups = lax.axis_size("dp")
    per_device, rows, units = unit_codes.shape
    slots = pair_list.shape[0] // n
    sets = offset_sets(n, slots)
    fits = (
        slots == groups
        and rows % 16 == 0
        and units % CHUNK == 0
        and CHUNK % (units // block_scales.shape[1]) == 0
        and units // block_scales.shape[1] % 128 == 0
        and units % (128 * groups) == 0
        and (groups * rows) % 128 == 0
    )
    if not sets or not fits:
        return general_body(unit_codes, block_scales, pair_list)
    columns = pair_list.T
    offsets = pair_list[:slots, 1] // per_device
    if slots == 4 and n > 4:
        free = [(sum(members) - 1 - n // 2 - (n - 1), at) for at, members in enumerate(sets)]
        side = lax.broadcasted_iota(jnp.int32, columns.shape, 0)
        slot = lax.broadcasted_iota(jnp.int32, columns.shape, 1)
        offsets = jnp.where((side == 1) & (slot < slots), columns // per_device, 0)
        branch = jnp.sum(sum(jnp.where(offsets == offset, at, 0) for offset, at in free))
        columns = jnp.where(side == 0, columns % per_device, columns)
        branch, columns = lax.optimization_barrier((branch, columns))
    else:
        branch = 0
        for at, members in enumerate(sets):
            same = jnp.all(jnp.any(offsets[:, None] == jnp.asarray(members)[None, :], axis=1))
            branch = branch + jnp.where(same, at, 0)
    calls = []
    for at, members in enumerate(sets):
        order, turns = TURNS.get(members, (members, (0,) * n)) if (n, groups) == (8, 4) else (members, (0,) * n)
        calls.append(functools.partial(pair_call, order, turns, n, groups, at))
    best = lax.switch(branch, calls, unit_codes, block_scales, columns)
    return (best[None, :slots], best[None, slots:])


def solution(mesh):
    in_specs = (P("expert", "dp", None), P("expert", None, "dp"), P())
    out_specs = (P("expert", None, "dp"), P("expert", None, "dp"))
    return jax.shard_map(body, mesh=mesh, in_specs=in_specs, out_specs=out_specs, check_vma=False)
```
